512 devices in a mesh: tm: 16 (over y, core), rows: 32 (over z, x).
Axes of the slice: x: 4, y: 8, z: 8, core: 2. Of those that a mesh axis runs over, the one named last changes fastest.
Arguments:
- latents: bfloat16 [64, 64, 64, 96], P('tm', 'rows'), may hold values from -6 to 6
- upstream: bfloat16 [64, 64, 64, 96], P('tm', 'rows'), may hold values from -6 to 6
- conv_one: bfloat16 [3, 3, 3, 96, 96], replicated, may hold values from -0.125 to 0.125
- conv_two: bfloat16 [3, 3, 3, 96, 96], replicated, may hold values from -0.125 to 0.125
Outputs:
- latent_grad: bfloat16 [64, 64, 64, 96], P('tm', 'rows')
- grad_one: float32 [3, 3, 3, 96, 96], replicated
- grad_two: float32 [3, 3, 3, 96, 96], replicated
The draws below stay inside these ranges and needn't reach their ends.
All inputs are finite; a program needn't handle non-finite values.
Results may differ from the reference program's by a relative error of at most 0.0058.
Values may be sent and summed in bfloat16 or wider, within the bound.
A program may use at most 64 MiB of HBM per device.

```python
import jax
import jax.numpy as jnp
from jax import lax

C = 96
WC = 64
TF = 64
NR = 64


def shard_levels(key, extent, pieces, low, high):
    gain, own = 1.0, jax.random.fold_in(key, 6)
    for position, shards_of in pieces:
        draws = jnp.exp(jax.random.uniform(jax.random.fold_in(own, position), (shards_of,), jnp.float32, low / len(pieces), high / len(pieces)))
        gain = gain * jnp.repeat(draws, extent[position] // shards_of).reshape([-1 if axis == position else 1 for axis in range(len(extent))])
    return gain


def scatter_about(key, extent, scale, bound, shards=(), held_as=jnp.bfloat16):
    result = scale * jax.random.normal(key, extent, jnp.float32)
    if shards:
        result = result * shard_levels(key, extent, shards, -0.22, 0.18)
    return jnp.clip(result, -bound, bound).astype(held_as)


def setup_inputs(seed: int = 0) -> dict:
    streams_of = jax.random.split(jax.random.key(seed), 5)
    latents = scatter_about(streams_of[0], (TF, NR, WC, C), 1.0, 6.0, ((0, 16), (1, 32)))
    upstream = scatter_about(streams_of[1], (TF, NR, WC, C), 1.0, 6.0, ((0, 16), (1, 32)))
    conv_one = scatter_about(streams_of[2], (3, 3, 3, C, C), (27 * C) ** -0.5, 0.125)
    conv_two = scatter_about(streams_of[3], (3, 3, 3, C, C), (27 * C) ** -0.5, 0.125)
    return dict(latents=latents, upstream=upstream, conv_one=conv_one, conv_two=conv_two)


def pad_cells(field):
    return jnp.pad(field, ((2, 0), (1, 1), (1, 1), (0, 0)))

def conv_full(padded, weight):
    return lax.conv_general_dilated(padded[None].astype(jnp.float32), weight.astype(jnp.float32), (1, 1, 1), 'VALID', dimension_numbers=('NDHWC', 'DHWIO', 'NDHWC'), precision=lax.Precision.HIGHEST)[0]

def silu_slope(value):
    sigma = jax.nn.sigmoid(value)
    return sigma * (1.0 + value * (1.0 - sigma))

def reference(latents, upstream, conv_one, conv_two):
    start = latents.astype(jnp.float32)
    first = jax.nn.silu(start).astype(jnp.bfloat16)
    pre_one = conv_full(pad_cells(first), conv_one)
    second = jax.nn.silu(pre_one).astype(jnp.bfloat16)
    _, pull_two = jax.vjp(conv_full, pad_cells(second).astype(jnp.float32), conv_two.astype(jnp.float32))
    pad_two, raw_two = pull_two(upstream.astype(jnp.float32))
    d_second = pad_two[2:, 1:-1, 1:-1]
    d_pre = (d_second * silu_slope(pre_one)).astype(jnp.bfloat16)
    _, pull_one = jax.vjp(conv_full, pad_cells(first).astype(jnp.float32), conv_one.astype(jnp.float32))
    pad_one, raw_one = pull_one(d_pre.astype(jnp.float32))
    d_first = pad_one[2:, 1:-1, 1:-1]
    latent_grad = (upstream.astype(jnp.float32) + d_first * silu_slope(start)).astype(jnp.bfloat16)
    scale = 1.0 / jnp.sqrt(jnp.float32(TF * NR * WC))
    return (latent_grad, raw_one * scale, raw_two * scale)
```

```python
import functools

import jax
import jax.numpy as jnp
from jax import lax
from jax.experimental import pallas as pl
from jax.experimental.pallas import tpu as pltpu
from jax.sharding import PartitionSpec as P

MESH = pl.DeviceIdType.MESH
F32, BF16 = jnp.float32, jnp.bfloat16
T, R, W, C, L = 4, 2, 64, 96, 128
CELLS = T * R * W
YN, ZN, XN = 8, 8, 4
ROWS = 2048
HALF = ROWS // 2
PART = HALF // 2
CHUNK = PART // 8
BLOCK = 224
FAR_FIRST = (4, 3, 5, 2, 6, 1, 7)


def silu(v):
    return v / (1.0 + jnp.exp(-v))


def silu_slope(v):
    s = 1.0 / (1.0 + jnp.exp(-v))
    return s * (1.0 + v * (1.0 - s))


def widen(v):
    return jnp.concatenate([v, jnp.zeros((v.shape[0], L - C), v.dtype)], axis=1)


def taps_of(ref):
    return [ref[a : a + T, b : b + R].reshape(CELLS, L) for a in range(3) for b in range(3)]


def spread(ref, weights):
    total = None
    for a in range(3):
        part = jnp.concatenate(
            [ref[a : a + T, b : b + R].reshape(CELLS, L) for b in range(3)], axis=1
        )
        term = jnp.dot(part, weights[a * 3 * L : (a + 1) * 3 * L, :], preferred_element_type=F32)
        total = term if total is None else total + term
    return total


def gather_columns(wide):
    column = lax.broadcasted_iota(jnp.int32, (CELLS, L), 0) % W
    low = jnp.where(column == 0, 0.0, pltpu.roll(wide[:, :L], 1, 0))
    high = jnp.where(column == W - 1, 0.0, pltpu.roll(wide[:, 2 * L :], CELLS - 1, 0))
    return low + wide[:, L : 2 * L] + high


def shifted_transposes(v):
    turned = v.T[:C]
    column = lax.broadcasted_iota(jnp.int32, (C, CELLS), 1) % W
    after = jnp.where(column == W - 1, 0.0, pltpu.roll(turned, CELLS - 1, 1))
    before = jnp.where(column == 0, 0.0, pltpu.roll(turned, 1, 1))
    return jnp.concatenate([after, turned, before], axis=0).astype(BF16)


def pack(grad):
    lane = lax.broadcasted_iota(jnp.int32, (72, L), 1)
    tail = grad[216:288]
    rows = []
    for k in range(3):
        moved = pltpu.roll(tail, (C - 32 * k) % L, 1) if k < 3 else tail
        rows.append(jnp.where(lane < C, grad[72 * k : 72 * k + 72], moved))
    return jnp.concatenate(rows, axis=0)


def unpack(held):
    lane = lax.broadcasted_iota(jnp.int32, (72, L), 1)
    parts = [
        pltpu.roll(held[72 * k : 72 * k + 72], (32 * k - C) % L, 1) for k in range(3)
    ]
    tail = jnp.where(lane < 32, parts[0], jnp.where(lane < 64, parts[1], parts[2]))
    return jnp.concatenate([held, tail], axis=0)


def kernel(
    lat, up, w1, w2, out_lat, out_one, out_two,
    fh, uh, dh, w1n, w1t, w2t, pre, dsec,
    mine, rc, held, r1, r2, r3, fin,
    hs, hr, cs, cr, s1, q1, s2, q2, s3, q3, s4, q4, s5, q5,
):
    tm, rw = lax.axis_index("tm"), lax.axis_index("rows")
    y, core, z, x = tm // 2, tm % 2, rw // XN, rw % XN

    def at(y2, c2, z2, x2):
        return (y2 * 2 + c2, z2 * XN + x2)

    def along(axis, k):
        if axis == "y":
            return at((y + k) % YN, core, z, x)
        if axis == "z":
            return at(y, core, (z + k) % ZN, x)
        return at(y, core, z, (x + k) % XN)

    def near(dt, dr):
        return ((tm + dt) % 16, (rw + dr) % 32)

    sibling = at(y, 1 - core, z, x)

    barrier = pltpu.get_barrier_semaphore()
    partners = [near(dt, dr) for dt in (-1, 0, 1) for dr in (-1, 0, 1) if (dt, dr) != (0, 0)]
    partners += [along("y", k) for k in range(1, YN)] + [along("z", k) for k in range(1, ZN)]
    partners += [along("x", k) for k in range(1, XN)] + [sibling]
    for who in partners:
        pl.semaphore_signal(barrier, inc=1, device_id=who, device_id_type=MESH)

    for t in range(T):
        for r in range(R):
            fh[t + 2, r + 1] = widen(silu(lat[t, r].astype(F32))).astype(BF16)
            uh[t, r + 1] = widen(up[t, r].astype(F32)).astype(BF16)
    pl.semaphore_wait(barrier, len(partners))

    def remote(src, dst, send, recv, who):
        copy = pltpu.make_async_remote_copy(
            src_ref=src, dst_ref=dst, send_sem=send, recv_sem=recv,
            device_id=who, device_id_type=MESH,
        )
        copy.start()
        return copy

    def halo(ref, own, frames, to, step, base):
        n = 0
        copies = []
        for dt, dr in ((step, -1), (step, 1), (step, 0), (0, -1), (0, 1)):
            fs = pl.ds(frames, 2) if dt else pl.ds(own, T)
            fd = pl.ds(to, 2) if dt else pl.ds(own, T)
            rs = pl.ds(1, 2) if dr == 0 else pl.ds(1 if dr < 0 else 2, 1)
            rd = pl.ds(1, 2) if dr == 0 else pl.ds(3 if dr < 0 else 0, 1)
            copies.append(
                remote(ref.at[fs, rs], ref.at[fd, rd], hs.at[base + n], hr.at[base + n], near(dt, dr))
            )
            n += 1
        return copies

    firsts = halo(fh, 2, 4, 0, 1, 0)
    ups = halo(uh, 0, 0, 4, -1, 5)

    w1n[...] = jnp.zeros_like(w1n)
    w1t[...] = jnp.zeros_like(w1t)
    w2t[...] = jnp.zeros_like(w2t)
    for a in range(3):
        for b in range(3):
            for e in range(3):
                tap = (a * 3 + b) * 3 + e
                row = (a * 3 + b) * L
                back = ((2 - a) * 3 + 2 - b) * L
                w1n[row : row + C, e * L : e * L + C] = w1[tap]
                w1t[back : back + C, (2 - e) * L : (2 - e) * L + C] = w1[tap].astype(F32).T.astype(BF16)
                w2t[back : back + C, (2 - e) * L : (2 - e) * L + C] = w2[tap].astype(F32).T.astype(BF16)
    mine[...] = jnp.zeros_like(mine)

    for copy in firsts:
        copy.wait_recv()

    @pl.when(tm == 0)
    def _():
        fh[0:2] = jnp.zeros((2, 4, W, L), BF16)

    def clear_rows(ref):
        @pl.when(rw == 0)
        def _():
            ref[:, 0] = jnp.zeros((6, W, L), BF16)

        @pl.when(rw == 31)
        def _():
            ref[:, 3] = jnp.zeros((6, W, L), BF16)

    def clear_late(ref):
        @pl.when(tm == 15)
        def _():
            ref[4:6] = jnp.zeros((2, 4, W, L), BF16)

    clear_rows(fh)
    pre[...] = gather_columns(spread(fh, w1n))
    for copy in ups:
        copy.wait_recv()
    clear_late(uh)
    clear_rows(uh)
    d_second = gather_columns(spread(uh, w2t))
    d_pre = (d_second * silu_slope(pre[...])).astype(BF16)
    dh[0:T, 1:3] = d_pre.reshape(T, R, W, L)
    for copy in ups + firsts:
        copy.wait_send()
    downs = halo(dh, 0, 0, 4, -1, 10)

    def weight_grad(field, ref, g):
        grad = jnp.dot(
            shifted_transposes(field), jnp.concatenate(taps_of(ref), axis=1), preferred_element_type=F32
        )
        for ab in range(9):
            mine[g, ab * BLOCK : ab * BLOCK + 216] = pack(grad[:, ab * L : ab * L + L]).astype(BF16)
        return remote(
            mine.at[g, pl.ds((1 - core) * HALF, HALF)], rc.at[g], cs.at[g], cr.at[g], sibling
        )

    first_axis, second_axis = ("z", "y"), ("y", "z")
    place = {"y": y, "z": z, "x": x}
    counts = {"y": YN, "z": ZN, "x": XN}

    def drain(ref, sem):
        pltpu.make_async_copy(ref, ref, sem).wait()

    def scatter(g, across):
        across.wait()
        held[g] = (
            mine[g, pl.ds(pl.multiple_of(core * HALF, HALF), HALF)].astype(F32) + rc[g].astype(F32)
        ).astype(BF16)
        for k in FAR_FIRST:
            for ab in range(2):
                axis = first_axis[ab]
                to = (place[axis] + k) % 8
                remote(
                    held.at[g, pl.ds(ab * PART + to * CHUNK, CHUNK)],
                    r1.at[g, ab, k - 1], s1.at[g, ab], q1.at[g, ab], along(axis, k),
                )

    def second_reduce(g):
        for ab in range(2):
            drain(r1.at[g, ab], q1.at[g, ab])
            here = place[first_axis[ab]]
            total = held[g, pl.ds(pl.multiple_of(ab * PART + here * CHUNK, CHUNK), CHUNK)].astype(F32)
            for k in range(7):
                total = total + r1[g, ab, k].astype(F32)
            axis = second_axis[ab]
            r2[g, ab, place[axis]] = total.astype(BF16)
            for k in FAR_FIRST:
                slot = r2.at[g, ab, place[axis]]
                remote(slot, slot, s2.at[g, ab], q2.at[g, ab], along(axis, k))

    def third_reduce(g):
        for ab in range(2):
            drain(r2.at[g, ab, pl.ds(0, 7)], q2.at[g, ab])
            total = r2[g, ab, 0].astype(F32)
            for k in range(1, 8):
                total = total + r2[g, ab, k].astype(F32)
            r3[g, ab, x] = total.astype(BF16)
            for k in (2, 1, 3):
                slot = r3.at[g, ab, x]
                remote(slot, slot, s3.at[g, ab], q3.at[g, ab], along("x", k))

    def gather(g):
        for ab in range(2):
            drain(r3.at[g, ab, pl.ds(0, 3)], q3.at[g, ab])
            total = r3[g, ab, 0].astype(F32)
            for k in range(1, 4):
                total = total + r3[g, ab, k].astype(F32)
            axis = first_axis[ab]
            base = core * HALF + ab * PART + place[axis] * CHUNK
            fin[g, pl.ds(pl.multiple_of(base, CHUNK), CHUNK)] = total.astype(BF16)
            for k in FAR_FIRST:
                spot = fin.at[g, pl.ds(base, CHUNK)]
                remote(spot, spot, s4.at[g, ab], q4.at[g, ab], along(axis, k))

    def cross(g):
        for ab in range(2):
            drain(fin.at[g, pl.ds(0, 7 * CHUNK)], q4.at[g, ab])
            spot = fin.at[g, pl.ds(core * HALF + ab * PART, PART)]
            remote(spot, spot, s5.at[g, ab], q5.at[g, ab], sibling)

    def finish(g, out):
        for ab in range(2):
            drain(fin.at[g, pl.ds(0, PART)], q5.at[g, ab])
        for ab in range(9):
            grad = unpack(fin[g, ab * BLOCK : ab * BLOCK + 216].astype(F32) * (1.0 / 512.0))
            a, b = ab // 3, ab % 3
            for e in range(3):
                out[((2 - a) * 3 + 2 - b) * 3 + 2 - e] = grad[e * C : e * C + C, :C]

    second = silu(pre[...]).astype(BF16).astype(F32)
    across_two = weight_grad(second, uh, 0)
    for copy in downs:
        copy.wait_recv()
    clear_late(dh)
    clear_rows(dh)
    scatter(0, across_two)
    first = fh[2:6, 1:3].reshape(CELLS, L).astype(F32)
    across_one = weight_grad(first, dh, 1)
    scatter(1, across_one)
    second_reduce(0)
    d_first = gather_columns(spread(dh, w1t))
    d_first = d_first.reshape(T, R, W, L)
    for t in range(T):
        for r in range(R):
            out_lat[t, r] = (
                up[t, r].astype(F32) + d_first[t, r][:, :C] * silu_slope(lat[t, r].astype(F32))
            ).astype(BF16)
    second_reduce(1)
    third_reduce(0)
    third_reduce(1)
    gather(0)
    gather(1)
    cross(0)
    finish(0, out_two)
    cross(1)
    finish(1, out_one)

    for copy in downs:
        copy.wait_send()
    for g in range(2):
        for ab in range(2):
            drain(r1.at[g, ab], s1.at[g, ab])
            drain(r2.at[g, ab, pl.ds(0, 7)], s2.at[g, ab])
            drain(r3.at[g, ab, pl.ds(0, 3)], s3.at[g, ab])
            drain(fin.at[g, pl.ds(0, 7 * CHUNK)], s4.at[g, ab])
            drain(fin.at[g, pl.ds(0, PART)], s5.at[g, ab])


def local(latents, upstream, conv_one, conv_two):
    vmem = pl.BlockSpec(memory_space=pltpu.VMEM)
    dma = pltpu.SemaphoreType.DMA
    pair = [dma((2, 2))] * 10
    grad = jax.ShapeDtypeStruct((27, C, C), F32)
    latent_grad, one, two = pl.pallas_call(
        kernel,
        out_shape=(jax.ShapeDtypeStruct(latents.shape, BF16), grad, grad),
        in_specs=[vmem] * 4,
        out_specs=[vmem] * 3,
        scratch_shapes=[
            pltpu.VMEM((6, 4, W, L), BF16),
            pltpu.VMEM((6, 4, W, L), BF16),
            pltpu.VMEM((6, 4, W, L), BF16),
            pltpu.VMEM((9 * L, 3 * L), BF16),
            pltpu.VMEM((9 * L, 3 * L), BF16),
            pltpu.VMEM((9 * L, 3 * L), BF16),
            pltpu.VMEM((CELLS, L), F32),
            pltpu.VMEM((CELLS, L), F32),
            pltpu.VMEM((2, ROWS, L), BF16),
            pltpu.VMEM((2, HALF, L), BF16),
            pltpu.VMEM((2, HALF, L), BF16),
            pltpu.VMEM((2, 2, 7, CHUNK, L), BF16),
            pltpu.VMEM((2, 2, 8, CHUNK, L), BF16),
            pltpu.VMEM((2, 2, 4, CHUNK, L), BF16),
            pltpu.VMEM((2, ROWS, L), BF16),
            dma((15,)),
            dma((15,)),
            dma((2,)),
            dma((2,)),
            *pair,
        ],
        compiler_params=pltpu.CompilerParams(
            collective_id=0, has_side_effects=True, vmem_limit_bytes=40 << 20
        ),
    )(latents, upstream, conv_one.reshape(27, C, C), conv_two.reshape(27, C, C))
    shape = (3, 3, 3, C, C)
    return latent_grad, one.reshape(shape), two.reshape(shape)


def solution(mesh):
    return jax.shard_map(
        local,
        mesh=mesh,
        in_specs=(P("tm", "rows", None, None), P("tm", "rows", None, None), P(), P()),
        out_specs=(P("tm", "rows", None, None), P(), P()),
        check_vma=False,
    )
```

```python
import functools

import jax
import jax.numpy as jnp
from jax import lax
from jax.experimental import pallas as pl
from jax.experimental.pallas import tpu as pltpu
from jax.sharding import PartitionSpec as P

MESH = pl.DeviceIdType.MESH
F32, BF16 = jnp.float32, jnp.bfloat16
T, R, W, C, L = 4, 2, 64, 96, 128
CELLS = T * R * W
YN, ZN, XN = 8, 8, 4
ROWS = 2048
HALF = ROWS // 2
PART = HALF // 2
CHUNK = PART // 8
BLOCK = 224
FAR_FIRST = (4, 3, 5, 2, 6, 1, 7)


def silu(v):
    return v / (1.0 + jnp.exp(-v))


def silu_slope(v):
    s = 1.0 / (1.0 + jnp.exp(-v))
    return s * (1.0 + v * (1.0 - s))


def widen(v):
    return jnp.concatenate([v, jnp.zeros((v.shape[0], L - C), v.dtype)], axis=1)


def taps_of(ref):
    return [ref[a : a + T, b : b + R].reshape(CELLS, L) for a in range(3) for b in range(3)]


def spread(ref, weights):
    total = None
    for a in range(3):
        part = jnp.concatenate(
            [ref[a : a + T, b : b + R].reshape(CELLS, L) for b in range(3)], axis=1
        )
        term = jnp.dot(part, weights[a * 3 * L : (a + 1) * 3 * L, :], preferred_element_type=F32)
        total = term if total is None else total + term
    return total


def gather_columns(wide):
    column = lax.broadcasted_iota(jnp.int32, (CELLS, L), 0) % W
    low = jnp.where(column == 0, 0.0, pltpu.roll(wide[:, :L], 1, 0))
    high = jnp.where(column == W - 1, 0.0, pltpu.roll(wide[:, 2 * L :], CELLS - 1, 0))
    return low + wide[:, L : 2 * L] + high


def shifted_transposes(v):
    turned = v.T[:C]
    column = lax.broadcasted_iota(jnp.int32, (C, CELLS), 1) % W
    after = jnp.where(column == W - 1, 0.0, pltpu.roll(turned, CELLS - 1, 1))
    before = jnp.where(column == 0, 0.0, pltpu.roll(turned, 1, 1))
    return jnp.concatenate([after, turned, before], axis=0).astype(BF16)


def pack(grad):
    lane = lax.broadcasted_iota(jnp.int32, (72, L), 1)
    tail = grad[216:288]
    rows = []
    for k in range(3):
        moved = pltpu.roll(tail, (C - 32 * k) % L, 1) if k < 3 else tail
        rows.append(jnp.where(lane < C, grad[72 * k : 72 * k + 72], moved))
    return jnp.concatenate(rows, axis=0)


def unpack(held):
    lane = lax.broadcasted_iota(jnp.int32, (72, L), 1)
    parts = [
        pltpu.roll(held[72 * k : 72 * k + 72], (32 * k - C) % L, 1) for k in range(3)
    ]
    tail = jnp.where(lane < 32, parts[0], jnp.where(lane < 64, parts[1], parts[2]))
    return jnp.concatenate([held, tail], axis=0)


def kernel(
    lat_in, up_in, w1_in, w2_in, out_lat, fin,
    lat, up, w1, w2,
    fh, uh, dh, w1n, w1t, w2t, pre, dsec,
    mine, rc, held, r1, r2, r3,
    lc, hs, hr, cs, cr, s1, q1, s2, q2, s3, q3, s4, q4, s5, q5,
):
    tm, rw = lax.axis_index("tm"), lax.axis_index("rows")
    y, core, z, x = tm // 2, tm % 2, rw // XN, rw % XN

    def at(y2, c2, z2, x2):
        return (y2 * 2 + c2, z2 * XN + x2)

    def along(axis, k):
        if axis == "y":
            return at((y + k) % YN, core, z, x)
        if axis == "z":
            return at(y, core, (z + k) % ZN, x)
        return at(y, core, z, (x + k) % XN)

    def near(dt, dr):
        return ((tm + dt) % 16, (rw + dr) % 32)

    sibling = at(y, 1 - core, z, x)

    fetches = [
        pltpu.make_async_copy(src, dst, lc.at[n])
        for n, (src, dst) in enumerate(((lat_in, lat), (up_in, up), (w1_in, w1), (w2_in, w2)))
    ]
    for fetch in fetches:
        fetch.start()

    barrier = pltpu.get_barrier_semaphore()
    partners = [near(dt, dr) for dt in (-1, 0, 1) for dr in (-1, 0, 1) if (dt, dr) != (0, 0)]
    partners += [along("y", k) for k in range(1, YN)] + [along("z", k) for k in range(1, ZN)]
    partners += [along("x", k) for k in range(1, XN)] + [sibling]
    for who in partners:
        pl.semaphore_signal(barrier, inc=1, device_id=who, device_id_type=MESH)

    fetches[0].wait()
    fetches[1].wait()
    for t in range(T):
        for r in range(R):
            fh[t + 2, r + 1] = widen(silu(lat[t, r].astype(F32))).astype(BF16)
            uh[t, r + 1] = widen(up[t, r].astype(F32)).astype(BF16)
    pl.semaphore_wait(barrier, len(partners))

    def remote(src, dst, send, recv, who):
        copy = pltpu.make_async_remote_copy(
            src_ref=src, dst_ref=dst, send_sem=send, recv_sem=recv,
            device_id=who, device_id_type=MESH,
        )
        copy.start()
        return copy

    def halo(ref, own, frames, to, step, base):
        n = 0
        copies = []
        for dt, dr in ((step, -1), (step, 1), (step, 0), (0, -1), (0, 1)):
            fs = pl.ds(frames, 2) if dt else pl.ds(own, T)
            fd = pl.ds(to, 2) if dt else pl.ds(own, T)
            rs = pl.ds(1, 2) if dr == 0 else pl.ds(1 if dr < 0 else 2, 1)
            rd = pl.ds(1, 2) if dr == 0 else pl.ds(3 if dr < 0 else 0, 1)
            copies.append(
                remote(ref.at[fs, rs], ref.at[fd, rd], hs.at[base + n], hr.at[base + n], near(dt, dr))
            )
            n += 1
        return copies

    firsts = halo(fh, 2, 4, 0, 1, 0)
    ups = halo(uh, 0, 0, 4, -1, 5)

    fetches[2].wait()
    fetches[3].wait()
    w1n[...] = jnp.zeros_like(w1n)
    w1t[...] = jnp.zeros_like(w1t)
    w2t[...] = jnp.zeros_like(w2t)
    for a in range(3):
        for b in range(3):
            for e in range(3):
                tap = (a * 3 + b) * 3 + e
                row = (a * 3 + b) * L
                back = ((2 - a) * 3 + 2 - b) * L
                w1n[row : row + C, e * L : e * L + C] = w1[tap]
                w1t[back : back + C, (2 - e) * L : (2 - e) * L + C] = w1[tap].astype(F32).T.astype(BF16)
                w2t[back : back + C, (2 - e) * L : (2 - e) * L + C] = w2[tap].astype(F32).T.astype(BF16)
    mine[...] = jnp.zeros_like(mine)

    for copy in firsts:
        copy.wait_recv()

    @pl.when(tm == 0)
    def _():
        fh[0:2] = jnp.zeros((2, 4, W, L), BF16)

    def clear_rows(ref):
        @pl.when(rw == 0)
        def _():
            ref[:, 0] = jnp.zeros((6, W, L), BF16)

        @pl.when(rw == 31)
        def _():
            ref[:, 3] = jnp.zeros((6, W, L), BF16)

    def clear_late(ref):
        @pl.when(tm == 15)
        def _():
            ref[4:6] = jnp.zeros((2, 4, W, L), BF16)

    clear_rows(fh)
    pre[...] = gather_columns(spread(fh, w1n))
    for copy in ups:
        copy.wait_recv()
    clear_late(uh)
    clear_rows(uh)
    d_second = gather_columns(spread(uh, w2t))
    d_pre = (d_second * silu_slope(pre[...])).astype(BF16)
    dh[0:T, 1:3] = d_pre.reshape(T, R, W, L)
    for copy in ups + firsts:
        copy.wait_send()
    downs = halo(dh, 0, 0, 4, -1, 10)

    def weight_grad(field, ref, g):
        grad = jnp.dot(
            shifted_transposes(field), jnp.concatenate(taps_of(ref), axis=1), preferred_element_type=F32
        )
        for ab in range(9):
            mine[g, ab * BLOCK : ab * BLOCK + 216] = pack(grad[:, ab * L : ab * L + L]).astype(BF16)
        return remote(
            mine.at[g, pl.ds((1 - core) * HALF, HALF)], rc.at[g], cs.at[g], cr.at[g], sibling
        )

    first_axis, second_axis = ("z", "y"), ("y", "z")
    place = {"y": y, "z": z, "x": x}
    counts = {"y": YN, "z": ZN, "x": XN}

    def drain(ref, sem):
        pltpu.make_async_copy(ref, ref, sem).wait()

    def scatter(g, across):
        across.wait()
        held[g] = (
            mine[g, pl.ds(pl.multiple_of(core * HALF, HALF), HALF)].astype(F32) + rc[g].astype(F32)
        ).astype(BF16)
        for k in FAR_FIRST:
            for ab in range(2):
                axis = first_axis[ab]
                to = (place[axis] + k) % 8
                remote(
                    held.at[g, pl.ds(ab * PART + to * CHUNK, CHUNK)],
                    r1.at[g, ab, k - 1], s1.at[g, ab], q1.at[g, ab], along(axis, k),
                )

    def second_reduce(g):
        for ab in range(2):
            drain(r1.at[g, ab], q1.at[g, ab])
            here = place[first_axis[ab]]
            total = held[g, pl.ds(pl.multiple_of(ab * PART + here * CHUNK, CHUNK), CHUNK)].astype(F32)
            for k in range(7):
                total = total + r1[g, ab, k].astype(F32)
            axis = second_axis[ab]
            r2[g, ab, place[axis]] = total.astype(BF16)
            for k in FAR_FIRST:
                slot = r2.at[g, ab, place[axis]]
                remote(slot, slot, s2.at[g, ab], q2.at[g, ab], along(axis, k))

    def third_reduce(g):
        for ab in range(2):
            drain(r2.at[g, ab, pl.ds(0, 7)], q2.at[g, ab])
            total = r2[g, ab, 0].astype(F32)
            for k in range(1, 8):
                total = total + r2[g, ab, k].astype(F32)
            r3[g, ab, x] = total.astype(BF16)
            for k in (2, 1, 3):
                slot = r3.at[g, ab, x]
                remote(slot, slot, s3.at[g, ab], q3.at[g, ab], along("x", k))

    def gather(g):
        for ab in range(2):
            drain(r3.at[g, ab, pl.ds(0, 3)], q3.at[g, ab])
            total = r3[g, ab, 0].astype(F32)
            for k in range(1, 4):
                total = total + r3[g, ab, k].astype(F32)
            axis = first_axis[ab]
            base = core * HALF + ab * PART + place[axis] * CHUNK
            fin[g, pl.ds(pl.multiple_of(base, CHUNK), CHUNK)] = total.astype(BF16)
            for k in FAR_FIRST:
                spot = fin.at[g, pl.ds(base, CHUNK)]
                remote(spot, spot, s4.at[g, ab], q4.at[g, ab], along(axis, k))

    def cross(g):
        for ab in range(2):
            drain(fin.at[g, pl.ds(0, 7 * CHUNK)], q4.at[g, ab])
            spot = fin.at[g, pl.ds(core * HALF + ab * PART, PART)]
            remote(spot, spot, s5.at[g, ab], q5.at[g, ab], sibling)

    second = silu(pre[...]).astype(BF16).astype(F32)
    across_two = weight_grad(second, uh, 0)
    for copy in downs:
        copy.wait_recv()
    clear_late(dh)
    clear_rows(dh)
    scatter(0, across_two)
    first = fh[2:6, 1:3].reshape(CELLS, L).astype(F32)
    across_one = weight_grad(first, dh, 1)
    scatter(1, across_one)
    second_reduce(0)
    d_first = gather_columns(spread(dh, w1t))
    d_first = d_first.reshape(T, R, W, L)
    for t in range(T):
        for r in range(R):
            out_lat[t, r] = (
                up[t, r].astype(F32) + d_first[t, r][:, :C] * silu_slope(lat[t, r].astype(F32))
            ).astype(BF16)
    second_reduce(1)
    third_reduce(0)
    third_reduce(1)
    gather(0)
    gather(1)
    cross(0)
    cross(1)
    for g in range(2):
        for ab in range(2):
            drain(fin.at[g, pl.ds(0, PART)], q5.at[g, ab])

    for copy in downs:
        copy.wait_send()
    for g in range(2):
        for ab in range(2):
            drain(r1.at[g, ab], s1.at[g, ab])
            drain(r2.at[g, ab, pl.ds(0, 7)], s2.at[g, ab])
            drain(r3.at[g, ab, pl.ds(0, 3)], s3.at[g, ab])
            drain(fin.at[g, pl.ds(0, 7 * CHUNK)], s4.at[g, ab])
            drain(fin.at[g, pl.ds(0, PART)], s5.at[g, ab])


def finish(fin, lat, out_lat, out_one, out_two, full, sems):
    copies = [pltpu.make_async_copy(lat, out_lat, sems.at[0])]
    copies[0].start()
    n = 1
    for g, out in ((0, out_two), (1, out_one)):
        for ab in range(9):
            grad = unpack(fin[g, ab * BLOCK : ab * BLOCK + 216].astype(F32) * (1.0 / 512.0))
            first = (8 - ab) * 3
            for e in range(3):
                full[g, first + 2 - e] = grad[e * C : e * C + C, :C]
            spot = pl.ds(first, 3)
            copies.append(pltpu.make_async_copy(full.at[g, spot], out.at[spot], sems.at[n]))
            copies[-1].start()
            n += 1
    for copy in copies:
        copy.wait()


def local(latents, upstream, conv_one, conv_two):
    vmem = pl.BlockSpec(memory_space=pltpu.VMEM)
    hbm = pl.BlockSpec(memory_space=pltpu.HBM)
    dma = pltpu.SemaphoreType.DMA
    pair = [dma((2, 2))] * 10
    grad = jax.ShapeDtypeStruct((27, C, C), F32)
    halo = pltpu.VMEM((6, 4, W, L), BF16)
    matrix = pltpu.VMEM((9 * L, 3 * L), BF16)
    latent_grad, packed = pl.pallas_call(
        kernel,
        out_shape=(
            jax.ShapeDtypeStruct(latents.shape, BF16),
            jax.ShapeDtypeStruct((2, ROWS, L), BF16),
        ),
        in_specs=[hbm] * 4,
        out_specs=[vmem] * 2,
        scratch_shapes=[
            pltpu.VMEM(latents.shape, BF16),
            pltpu.VMEM(latents.shape, BF16),
            pltpu.VMEM((27, C, C), BF16),
            pltpu.VMEM((27, C, C), BF16),
            halo,
            halo,
            halo,
            matrix,
            matrix,
            matrix,
            pltpu.VMEM((CELLS, L), F32),
            pltpu.VMEM((CELLS, L), F32),
            pltpu.VMEM((2, ROWS, L), BF16),
            pltpu.VMEM((2, HALF, L), BF16),
            pltpu.VMEM((2, HALF, L), BF16),
            pltpu.VMEM((2, 2, 7, CHUNK, L), BF16),
            pltpu.VMEM((2, 2, 8, CHUNK, L), BF16),
            pltpu.VMEM((2, 2, 4, CHUNK, L), BF16),
            dma((4,)),
            dma((15,)),
            dma((15,)),
            dma((2,)),
            dma((2,)),
            *pair,
        ],
        compiler_params=pltpu.CompilerParams(
            collective_id=0, has_side_effects=True, vmem_limit_bytes=60 << 20
        ),
    )(latents, upstream, conv_one.reshape(27, C, C), conv_two.reshape(27, C, C))
    latent_grad, one, two = pl.pallas_call(
        finish,
        out_shape=(jax.ShapeDtypeStruct(latents.shape, BF16), grad, grad),
        in_specs=[vmem] * 2,
        out_specs=[hbm] * 3,
        scratch_shapes=[pltpu.VMEM((2, 27, C, C), F32), dma((19,))],
        compiler_params=pltpu.CompilerParams(vmem_limit_bytes=24 << 20),
    )(packed, latent_grad)
    shape = (3, 3, 3, C, C)
    return latent_grad, one.reshape(shape), two.reshape(shape)


def solution(mesh):
    return jax.shard_map(
        local,
        mesh=mesh,
        in_specs=(P("tm", "rows", None, None), P("tm", "rows", None, None), P(), P()),
        out_specs=(P("tm", "rows", None, None), P(), P()),
        check_vma=False,
    )
```

```python
import functools

import jax
import jax.numpy as jnp
from jax import lax
from jax.experimental import pallas as pl
from jax.experimental.pallas import tpu as pltpu
from jax.sharding import PartitionSpec as P

MESH = pl.DeviceIdType.MESH
F32, BF16 = jnp.float32, jnp.bfloat16
T, R, W, C, L = 4, 2, 64, 96, 128
CELLS = T * R * W
YN, ZN, XN = 8, 8, 4
ROWS = 2048
HALF = ROWS // 2
CHUNK = HALF // 8
SHARE = CHUNK // XN
BLOCK = 224
FAR_FIRST = (4, 3, 5, 2, 6, 1, 7)


def silu(v):
    return v / (1.0 + jnp.exp(-v))


def silu_slope(v):
    s = 1.0 / (1.0 + jnp.exp(-v))
    return s * (1.0 + v * (1.0 - s))


def widen(v):
    return jnp.concatenate([v, jnp.zeros((v.shape[0], L - C), v.dtype)], axis=1)


def taps_of(ref):
    return [ref[a : a + T, b : b + R].reshape(CELLS, L) for a in range(3) for b in range(3)]


def spread(ref, weights, turned=False):
    total = None
    for a in range(3):
        part = jnp.concatenate(
            [ref[a : a + T, b : b + R].reshape(CELLS, L) for b in range(3)], axis=1
        )
        if turned:
            matrix, depth = weights[:, a * 3 * L : (a + 1) * 3 * L], 1
        else:
            matrix, depth = weights[a * 3 * L : (a + 1) * 3 * L, :], 0
        term = lax.dot_general(
            part, matrix, (((1,), (depth,)), ((), ())), preferred_element_type=F32
        )
        total = term if total is None else total + term
    return total


def gather_columns(wide):
    column = lax.broadcasted_iota(jnp.int32, (CELLS, L), 0) % W
    low = jnp.where(column == 0, 0.0, pltpu.roll(wide[:, :L], 1, 0))
    high = jnp.where(column == W - 1, 0.0, pltpu.roll(wide[:, 2 * L :], CELLS - 1, 0))
    return low + wide[:, L : 2 * L] + high


def shifted_transposes(v):
    turned = v.T[:C]
    column = lax.broadcasted_iota(jnp.int32, (C, CELLS), 1) % W
    after = jnp.where(column == W - 1, 0.0, pltpu.roll(turned, CELLS - 1, 1))
    before = jnp.where(column == 0, 0.0, pltpu.roll(turned, 1, 1))
    return jnp.concatenate([after, turned, before], axis=0).astype(BF16)


def pack(grad):
    lane = lax.broadcasted_iota(jnp.int32, (72, L), 1)
    tail = grad[216:288]
    rows = []
    for k in range(3):
        moved = pltpu.roll(tail, (C - 32 * k) % L, 1)
        rows.append(jnp.where(lane < C, grad[72 * k : 72 * k + 72], moved))
    rows.append(jnp.zeros((BLOCK - 216, L), F32))
    return jnp.concatenate(rows, axis=0)


def unpack(held):
    lane = lax.broadcasted_iota(jnp.int32, (72, L), 1)
    parts = [
        pltpu.roll(held[72 * k : 72 * k + 72], (32 * k - C) % L, 1) for k in range(3)
    ]
    tail = jnp.where(lane < 32, parts[0], jnp.where(lane < 64, parts[1], parts[2]))
    return jnp.concatenate([held, tail], axis=0)


def kernel(
    lat_in, up_in, w1_in, w2_in, lat_out, packed,
    lat, up, w1, w2, out_lat,
    fh, uh, dh, ft, w1n, w1t, w2t, pre,
    mine, rc, held, part, r1, r2, r3, fin,
    lc, oc, hs, hr, cs, cr, s1, q1, s2, q2, s3, q3, s4, q4, s5, q5, s6, q6, two_away, four_away,
):
    tm, rw = lax.axis_index("tm"), lax.axis_index("rows")
    y, core, z, x = tm // 2, tm % 2, rw // XN, rw % XN

    def at(y2, c2, z2, x2):
        return ((y2 % YN) * 2 + c2, (z2 % ZN) * XN + x2 % XN)

    def near(dt, dr):
        return ((tm + dt) % 16, (rw + dr) % 32)

    def first_ring(k):
        return at(y + k * core, core, z + k * (1 - core), x)

    def second_ring(k):
        return at(y + k * (1 - core), core, z + k * core, x)

    def third_ring(k):
        return at(y, core, z, x + k)

    p = z + core * (y - z)
    q = y + core * (z - y)
    sibling = at(y, 1 - core, z, x)

    fetches = [
        pltpu.make_async_copy(src, dst, lc.at[n])
        for n, (src, dst) in enumerate(((lat_in, lat), (up_in, up), (w1_in, w1), (w2_in, w2)))
    ]
    for fetch in fetches:
        fetch.start()

    def greet(semaphore, partners):
        for who in partners:
            pl.semaphore_signal(semaphore, inc=1, device_id=who, device_id_type=MESH)

    barrier = pltpu.get_barrier_semaphore()
    around = [near(dt, dr) for dt in (-1, 0, 1) for dr in (-1, 0, 1) if (dt, dr) != (0, 0)]
    ones = [at(y - 1, core, z, x), at(y + 1, core, z, x), at(y, core, z - 1, x), at(y, core, z + 1, x)]
    ones += [at(y, core, z, x - 1), at(y, core, z, x + 1)]
    twos = [at(y - 2, core, z, x), at(y + 2, core, z, x), at(y, core, z - 2, x), at(y, core, z + 2, x)]
    greet(barrier, around + ones)

    fetches[0].wait()
    for t in range(T):
        for r in range(R):
            fh[t + 2, r + 1] = widen(silu(lat[t, r].astype(F32))).astype(BF16)
    fetches[1].wait()
    for t in range(T):
        for r in range(R):
            uh[t, r + 1] = widen(up[t, r].astype(F32)).astype(BF16)
    pl.semaphore_wait(barrier, len(around) + len(ones))

    def remote(src, dst, send, recv, who):
        copy = pltpu.make_async_remote_copy(
            src_ref=src, dst_ref=dst, send_sem=send, recv_sem=recv,
            device_id=who, device_id_type=MESH,
        )
        copy.start()
        return copy

    def halo(ref, own, frames, to, step, base):
        copies = []
        for n, (dt, dr) in enumerate(((step, -1), (step, 1), (0, -1), (0, 1), (step, 0))):
            fs = pl.ds(frames, 2) if dt else pl.ds(own, T)
            fd = pl.ds(to, 2) if dt else pl.ds(own, T)
            rs = pl.ds(1, 2) if dr == 0 else pl.ds(1 if dr < 0 else 2, 1)
            rd = pl.ds(1, 2) if dr == 0 else pl.ds(3 if dr < 0 else 0, 1)
            copies.append(
                remote(ref.at[fs, rs], ref.at[fd, rd], hs.at[base + n], hr.at[base + n], near(dt, dr))
            )
        return copies

    firsts = halo(fh, 2, 4, 0, 1, 0)
    ups = halo(uh, 0, 0, 4, -1, 5)
    greet(two_away, ones)

    def place_taps(matrix, source, turned):
        matrix[...] = jnp.zeros_like(matrix)
        for a in range(3):
            for b in range(3):
                for e in range(3):
                    row, lane = (a * 3 + b) * L, e * L
                    if turned:
                        row, lane = (2 - e) * L, ((2 - a) * 3 + 2 - b) * L
                    matrix[row : row + C, lane : lane + C] = source[(a * 3 + b) * 3 + e]

    fetches[2].wait()
    place_taps(w1n, w1, False)
    fetches[3].wait()
    place_taps(w2t, w2, True)
    mine[:, 9 * BLOCK :] = jnp.zeros((2, ROWS - 9 * BLOCK, L), BF16)
    pl.semaphore_wait(two_away, len(ones))
    greet(four_away, twos)

    def clear_rows(ref):
        @pl.when(rw == 0)
        def _():
            ref[:, 0] = jnp.zeros((6, W, L), BF16)

        @pl.when(rw == 31)
        def _():
            ref[:, 3] = jnp.zeros((6, W, L), BF16)

    def clear_late(ref):
        @pl.when(tm == 15)
        def _():
            ref[4:6] = jnp.zeros((2, 4, W, L), BF16)

    for copy in firsts:
        copy.wait_recv()

    @pl.when(tm == 0)
    def _():
        fh[0:2] = jnp.zeros((2, 4, W, L), BF16)

    clear_rows(fh)
    pre[...] = gather_columns(spread(fh, w1n))
    for b in range(3):
        ft[b] = fh[:, b : b + R].reshape(6 * R * W, L).astype(F32).T[:C].astype(BF16)
    for copy in ups:
        copy.wait_recv()
    clear_late(uh)
    clear_rows(uh)

    def cross_cores(g):
        return remote(
            mine.at[g, pl.ds((1 - core) * HALF, HALF)], rc.at[g], cs.at[g], cr.at[g], sibling
        )

    second = silu(pre[...]).astype(BF16).astype(F32)
    grad = jnp.dot(
        shifted_transposes(second), jnp.concatenate(taps_of(uh), axis=1), preferred_element_type=F32
    )
    for n in range(9):
        mine[0, n * BLOCK : (n + 1) * BLOCK] = pack(grad[:, n * L : n * L + L]).astype(BF16)
    across_two = cross_cores(0)

    d_second = gather_columns(spread(uh, w2t, True))
    d_pre = (d_second * silu_slope(pre[...])).astype(BF16)
    dh[0:T, 1:3] = d_pre.reshape(T, R, W, L)
    downs = halo(dh, 0, 0, 4, -1, 10)

    d_pre = d_pre.astype(F32)
    column = lax.broadcasted_iota(jnp.int32, (CELLS, L), 0) % W
    after = jnp.where(column == W - 1, 0.0, pltpu.roll(d_pre, CELLS - 1, 0))
    before = jnp.where(column == 0, 0.0, pltpu.roll(d_pre, 1, 0))
    moved = jnp.concatenate([after, d_pre, before], axis=1).astype(BF16)
    field = jnp.concatenate(
        [ft[b, :, a * R * W : a * R * W + CELLS] for a in range(3) for b in range(3)], axis=0
    )
    grad = jnp.dot(field, moved, preferred_element_type=F32)
    for a in range(3):
        for e in range(3):
            n = a * 3 + e
            mine[1, n * BLOCK : (n + 1) * BLOCK] = pack(
                grad[a * 3 * C : (a + 1) * 3 * C, e * L : e * L + L]
            ).astype(BF16)
    across_one = cross_cores(1)

    def drain(ref, sem):
        pltpu.make_async_copy(ref, ref, sem).wait()

    def total_of(parts):
        total = parts[0].astype(F32)
        for part in parts[1:]:
            total = total + part.astype(F32)
        return total

    def rows_at(start):
        return pl.ds(pl.multiple_of(start, CHUNK), CHUNK)

    def scatter(g, across):
        across.wait_recv()
        for k in FAR_FIRST + (0,):
            to = rows_at((p + k) % 8 * CHUNK)
            from_mine = rows_at(core * HALF + (p + k) % 8 * CHUNK)
            held[g, to] = total_of([mine[g, from_mine], rc[g, to]]).astype(BF16)
            if k:
                remote(held.at[g, to], r1.at[g, k - 1], s1.at[g], q1.at[g], first_ring(k))

    def second_scatter(g):
        drain(r1.at[g], q1.at[g])
        total = total_of([held[g, rows_at(p * CHUNK)]] + [r1[g, k] for k in range(7)])
        part[g] = total.astype(BF16)
        for k in (2, 1, 3):
            spot = part.at[g, pl.ds(pl.multiple_of((x + k) % XN * SHARE, SHARE), SHARE)]
            remote(spot, r3.at[g, k - 1], s3.at[g], q3.at[g], third_ring(k))

    def second_reduce(g):
        drain(r3.at[g], q3.at[g])
        mine_of = part[g, pl.ds(pl.multiple_of(x * SHARE, SHARE), SHARE)]
        slot = r2.at[g, q]
        slot[...] = total_of([mine_of] + [r3[g, k] for k in range(3)]).astype(BF16)
        for k in FAR_FIRST:
            remote(slot, slot, s2.at[g], q2.at[g], second_ring(k))

    def third_gather(g):
        drain(r2.at[g, pl.ds(0, 7)], q2.at[g])
        start = core * HALF + p * CHUNK + x * SHARE
        spot = fin.at[g, pl.ds(pl.multiple_of(start, SHARE), SHARE)]
        spot[...] = total_of([r2[g, k] for k in range(8)]).astype(BF16)
        for k in (2, 1, 3):
            remote(spot, spot, s6.at[g], q6.at[g], third_ring(k))

    def gather(g):
        drain(fin.at[g, pl.ds(0, 3 * SHARE)], q6.at[g])
        spot = fin.at[g, rows_at(core * HALF + p * CHUNK)]
        for k in FAR_FIRST:
            remote(spot, spot, s4.at[g], q4.at[g], first_ring(k))

    def half_of(g, c):
        return fin.at[g, pl.ds(pl.multiple_of(c * HALF, HALF), HALF)]

    def store(g, c, n):
        spot = packed.at[g, pl.ds(pl.multiple_of(c * HALF, HALF), HALF)]
        copy = pltpu.make_async_copy(half_of(g, c), spot, oc.at[2 * g + n])
        copy.start()
        return copy

    def cross_back(g):
        drain(fin.at[g, pl.ds(0, 7 * CHUNK)], q4.at[g])
        remote(half_of(g, core), half_of(g, core), s5.at[g], q5.at[g], sibling)
        return store(g, core, 0)

    def complete(g):
        drain(half_of(g, 1 - core), q5.at[g])
        return store(g, 1 - core, 1)

    pl.semaphore_wait(four_away, len(twos))
    scatter(0, across_two)
    scatter(1, across_one)
    place_taps(w1t, w1, True)
    second_scatter(0)
    second_scatter(1)
    second_reduce(0)
    second_reduce(1)
    for copy in downs:
        copy.wait_recv()
    clear_late(dh)
    clear_rows(dh)
    d_first = gather_columns(spread(dh, w1t, True)).reshape(T, R, W, L)
    for t in range(T):
        for r in range(R):
            out_lat[t, r] = (
                up[t, r].astype(F32) + d_first[t, r][:, :C] * silu_slope(lat[t, r].astype(F32))
            ).astype(BF16)
    stores = [pltpu.make_async_copy(out_lat, lat_out, oc.at[4])]
    stores[0].start()
    third_gather(0)
    third_gather(1)
    gather(0)
    gather(1)
    stores.append(cross_back(0))
    stores.append(cross_back(1))
    stores.append(complete(0))
    stores.append(complete(1))

    for copy in firsts + ups + downs + [across_two, across_one]:
        copy.wait_send()
    for g in range(2):
        drain(r1.at[g], s1.at[g])
        drain(r2.at[g, pl.ds(0, 7)], s2.at[g])
        drain(r3.at[g], s3.at[g])
        drain(fin.at[g, pl.ds(0, 3 * SHARE)], s6.at[g])
        drain(fin.at[g, pl.ds(0, 7 * CHUNK)], s4.at[g])
        drain(half_of(g, core), s5.at[g])
    for copy in stores:
        copy.wait()


def finish(packed, lat, out_lat, out_one, out_two, held, full, carried, ins, outs):
    fetches = []
    for n in range(18):
        spot = pl.ds(n % 9 * BLOCK, BLOCK)
        fetches.append(
            pltpu.make_async_copy(packed.at[n // 9, spot], held.at[n // 9, spot], ins.at[n])
        )
        fetches[-1].start()
    carried_in = pltpu.make_async_copy(lat, carried, ins.at[18])
    carried_in.start()
    copies = []

    def widened(g, n):
        fetches[g * 9 + n].wait()
        return unpack(held[g, n * BLOCK : n * BLOCK + 216].astype(F32) * (1.0 / 512.0))

    def write(g, out, first, count):
        spot = pl.ds(first, count)
        copies.append(pltpu.make_async_copy(full.at[g, spot], out.at[spot], outs.at[len(copies)]))
        copies[-1].start()

    for n in range(9):
        grad = widened(0, n)
        first = (8 - n) * 3
        for e in range(3):
            full[0, first + 2 - e] = grad[e * C : e * C + C, :C]
        write(0, out_two, first, 3)
    carried_in.wait()
    copies.append(pltpu.make_async_copy(carried, out_lat, outs.at[9]))
    copies[-1].start()
    for a in range(3):
        for e in range(3):
            grad = widened(1, a * 3 + e)
            for b in range(3):
                full[1, (a * 3 + b) * 3 + e] = grad[b * C : b * C + C, :C]
        write(1, out_one, a * 9, 9)
    for copy in copies:
        copy.wait()


def local(latents, upstream, conv_one, conv_two):
    hbm = pl.BlockSpec(memory_space=pltpu.HBM)
    dma = pltpu.SemaphoreType.DMA
    grad = jax.ShapeDtypeStruct((27, C, C), F32)
    field = pltpu.VMEM(latents.shape, BF16)
    taps = pltpu.VMEM((27, C, C), BF16)
    halo = pltpu.VMEM((6, 4, W, L), BF16)
    matrix = pltpu.VMEM((9 * L, 3 * L), BF16)
    turned = pltpu.VMEM((3 * L, 9 * L), BF16)
    params = functools.partial(pltpu.CompilerParams, vmem_limit_bytes=60 << 20)
    latent_grad, packed = pl.pallas_call(
        kernel,
        out_shape=(
            jax.ShapeDtypeStruct(latents.shape, BF16),
            jax.ShapeDtypeStruct((2, ROWS, L), BF16),
        ),
        in_specs=[hbm] * 4,
        out_specs=[hbm] * 2,
        scratch_shapes=[
            field,
            field,
            taps,
            taps,
            field,
            halo,
            halo,
            halo,
            pltpu.VMEM((3, C, 6 * R * W), BF16),
            matrix,
            turned,
            turned,
            pltpu.VMEM((CELLS, L), F32),
            pltpu.VMEM((2, ROWS, L), BF16),
            pltpu.VMEM((2, HALF, L), BF16),
            pltpu.VMEM((2, HALF, L), BF16),
            pltpu.VMEM((2, CHUNK, L), BF16),
            pltpu.VMEM((2, 7, CHUNK, L), BF16),
            pltpu.VMEM((2, 8, SHARE, L), BF16),
            pltpu.VMEM((2, 3, SHARE, L), BF16),
            pltpu.VMEM((2, ROWS, L), BF16),
            dma((4,)),
            dma((5,)),
            dma((15,)),
            dma((15,)),
            *[dma((2,))] * 14,
            pltpu.SemaphoreType.REGULAR,
            pltpu.SemaphoreType.REGULAR,
        ],
        compiler_params=params(collective_id=0, has_side_effects=True),
    )(latents, upstream, conv_one.reshape(27, C, C), conv_two.reshape(27, C, C))
    latent_grad, one, two = pl.pallas_call(
        finish,
        out_shape=(jax.ShapeDtypeStruct(latents.shape, BF16), grad, grad),
        in_specs=[hbm] * 2,
        out_specs=[hbm] * 3,
        scratch_shapes=[
            pltpu.VMEM((2, ROWS, L), BF16),
            pltpu.VMEM((2, 27, C, C), F32),
            field,
            dma((19,)),
            dma((13,)),
        ],
        compiler_params=params(),
    )(packed, latent_grad)
    shape = (3, 3, 3, C, C)
    return latent_grad, one.reshape(shape), two.reshape(shape)


def solution(mesh):
    return jax.shard_map(
        local,
        mesh=mesh,
        in_specs=(P("tm", "rows", None, None), P("tm", "rows", None, None), P(), P()),
        out_specs=(P("tm", "rows", None, None), P(), P()),
        check_vma=False,
    )
```

```python
import functools

import jax
import jax.numpy as jnp
from jax import lax
from jax.experimental import pallas as pl
from jax.experimental.pallas import tpu as pltpu
from jax.sharding import PartitionSpec as P

MESH = pl.DeviceIdType.MESH
F32, BF16 = jnp.float32, jnp.bfloat16
T, R, W, C, L = 4, 2, 64, 96, 128
CELLS = T * R * W
YN, ZN, XN = 8, 8, 4
ROWS = 2048
HALF = ROWS // 2
PART = HALF // 2
CHUNK = PART // 8
WIDE = PART // XN
SHARE = CHUNK // XN
BLOCK = 224
FAR_FIRST = (4, 3, 5, 2, 6, 1, 7)


def silu(v):
    return v / (1.0 + jnp.exp(-v))


def silu_slope(v):
    s = 1.0 / (1.0 + jnp.exp(-v))
    return s * (1.0 + v * (1.0 - s))


def widen(v):
    return jnp.concatenate([v, jnp.zeros((v.shape[0], L - C), v.dtype)], axis=1)


def taps_of(ref):
    return [ref[a : a + T, b : b + R].reshape(CELLS, L) for a in range(3) for b in range(3)]


def spread(ref, weights, turned=False):
    total = None
    for a in range(3):
        part = jnp.concatenate(
            [ref[a : a + T, b : b + R].reshape(CELLS, L) for b in range(3)], axis=1
        )
        if turned:
            matrix, depth = weights[:, a * 3 * L : (a + 1) * 3 * L], 1
        else:
            matrix, depth = weights[a * 3 * L : (a + 1) * 3 * L, :], 0
        term = lax.dot_general(
            part, matrix, (((1,), (depth,)), ((), ())), preferred_element_type=F32
        )
        total = term if total is None else total + term
    return total


def gather_columns(wide):
    column = lax.broadcasted_iota(jnp.int32, (CELLS, L), 0) % W
    low = jnp.where(column == 0, 0.0, pltpu.roll(wide[:, :L], 1, 0))
    high = jnp.where(column == W - 1, 0.0, pltpu.roll(wide[:, 2 * L :], CELLS - 1, 0))
    return low + wide[:, L : 2 * L] + high


def shifted_transposes(v):
    turned = v.T[:C]
    column = lax.broadcasted_iota(jnp.int32, (C, CELLS), 1) % W
    after = jnp.where(column == W - 1, 0.0, pltpu.roll(turned, CELLS - 1, 1))
    before = jnp.where(column == 0, 0.0, pltpu.roll(turned, 1, 1))
    return jnp.concatenate([after, turned, before], axis=0).astype(BF16)


def pack(grad):
    lane = lax.broadcasted_iota(jnp.int32, (72, L), 1)
    tail = grad[216:288]
    rows = []
    for k in range(3):
        moved = pltpu.roll(tail, (C - 32 * k) % L, 1)
        rows.append(jnp.where(lane < C, grad[72 * k : 72 * k + 72], moved))
    rows.append(jnp.zeros((BLOCK - 216, L), F32))
    return jnp.concatenate(rows, axis=0)


def unpack(held):
    lane = lax.broadcasted_iota(jnp.int32, (72, L), 1)
    parts = [
        pltpu.roll(held[72 * k : 72 * k + 72], (32 * k - C) % L, 1) for k in range(3)
    ]
    tail = jnp.where(lane < 32, parts[0], jnp.where(lane < 64, parts[1], parts[2]))
    return jnp.concatenate([held, tail], axis=0)


def kernel(
    lat_in, up_in, w1_in, w2_in, lat_out, packed,
    lat, up, w1, w2, out_lat,
    fh, uh, dh, ft, st, w1n, w1t, w2t, pre,
    mine, rc, held, pa, pb, a1, b1, a2, b2, c2, fin,
    lc, oc, hs, hr, cs, cr, s1, q1, s2, q2, s4, q4, s6, q6, s3, q3, s5, q5, *waves,
):
    tm, rw = lax.axis_index("tm"), lax.axis_index("rows")
    y, core, z, x = tm // 2, tm % 2, rw // XN, rw % XN

    def at(y2, c2, z2, x2):
        return ((y2 % YN) * 2 + c2, (z2 % ZN) * XN + x2 % XN)

    def near(dt, dr):
        return ((tm + dt) % 16, (rw + dr) % 32)

    def first_ring(k):
        return at(y + k * core, core, z + k * (1 - core), x)

    def second_ring(k):
        return at(y + k * (1 - core), core, z + k * core, x)

    def third_ring(k):
        return at(y, core, z, x + k)

    p = z + core * (y - z)
    q = y + core * (z - y)
    sibling = at(y, 1 - core, z, x)

    def greet(semaphore, partners):
        for who in partners:
            pl.semaphore_signal(semaphore, inc=1, device_id=who, device_id_type=MESH)

    barrier = pltpu.get_barrier_semaphore()
    around = [near(dt, dr) for dt, dr in ((-1, -1), (-1, 1), (1, -1), (1, 1), (0, -1), (0, 1), (-1, 0), (1, 0))]
    ones = [at(y - 1, core, z, x), at(y + 1, core, z, x), at(y, core, z - 1, x), at(y, core, z + 1, x)]
    ones += [at(y, core, z, x - 1), at(y, core, z, x + 1)]
    twos = [at(y - 2, core, z, x), at(y + 2, core, z, x), at(y, core, z - 2, x), at(y, core, z + 2, x)]
    greet(barrier, around + ones)

    fetches = [
        pltpu.make_async_copy(src, dst, lc.at[n])
        for n, (src, dst) in enumerate(
            (
                (lat_in, lat.at[pl.ds(2, T), pl.ds(1, R)]),
                (up_in, up.at[pl.ds(0, T), pl.ds(1, R)]),
                (w1_in, w1),
                (w2_in, w2),
            )
        )
    ]
    for fetch in fetches:
        fetch.start()

    def remote(src, dst, send, recv, who):
        copy = pltpu.make_async_remote_copy(
            src_ref=src, dst_ref=dst, send_sem=send, recv_sem=recv,
            device_id=who, device_id_type=MESH,
        )
        copy.start()
        return copy

    def halo(src, corner, dst, own, lead, to, step, base):
        copies = []
        for n, (dt, dr) in enumerate(((step, -1), (step, 1), (0, -1), (0, 1), (step, 0))):
            fs = pl.ds(corner[0] + lead, 2) if dt else pl.ds(corner[0], T)
            fd = pl.ds(to, 2) if dt else pl.ds(own, T)
            rs = pl.ds(corner[1], 2) if dr == 0 else pl.ds(corner[1] + (dr > 0), 1)
            rd = pl.ds(1, 2) if dr == 0 else pl.ds(3 if dr < 0 else 0, 1)
            copies.append(
                remote(src.at[fs, rs], dst.at[fd, rd], hs.at[base + n], hr.at[base + n], near(dt, dr))
            )
        return copies

    def take_lat(f, r):
        fh[f, r] = widen(silu(lat[f, r].astype(F32))).astype(BF16)

    def take_up(f, r):
        uh[f, r] = widen(up[f, r])

    lines = [(f, r) for f in range(6) for r in range(4)]
    own_lat = [(f, r) for f, r in lines if f >= 2 and r in (1, 2)]
    own_up = [(f, r) for f, r in lines if f < T and r in (1, 2)]
    fetches[0].wait()
    for line in own_lat:
        take_lat(*line)
    fetches[1].wait()
    for line in own_up:
        take_up(*line)
    pl.semaphore_wait(barrier, len(around) + len(ones))
    firsts = halo(fh, (2, 1), fh, 2, 2, 0, 1, 0)
    ups = halo(uh, (0, 1), uh, 0, 0, 4, -1, 5)
    greet(waves[0], ones)

    def place_taps(matrix, source, turned):
        matrix[...] = jnp.zeros_like(matrix)
        for a in range(3):
            for b in range(3):
                for e in range(3):
                    row, lane = (a * 3 + b) * L, e * L
                    if turned:
                        row, lane = (2 - e) * L, ((2 - a) * 3 + 2 - b) * L
                    matrix[row : row + C, lane : lane + C] = source[(a * 3 + b) * 3 + e]

    fetches[2].wait()
    place_taps(w1n, w1, False)
    fetches[3].wait()
    place_taps(w2t, w2, True)
    mine[:, 9 * BLOCK :] = jnp.zeros((2, ROWS - 9 * BLOCK, L), BF16)
    pl.semaphore_wait(waves[0], len(ones))
    greet(waves[1], twos)

    def clear_rows(ref):
        @pl.when(rw == 0)
        def _():
            ref[:, 0] = jnp.zeros((6, W, L), BF16)

        @pl.when(rw == 31)
        def _():
            ref[:, 3] = jnp.zeros((6, W, L), BF16)

    def clear_late(ref):
        @pl.when(tm == 15)
        def _():
            ref[4:6] = jnp.zeros((2, 4, W, L), BF16)

    for copy in firsts:
        copy.wait_recv()

    @pl.when(tm == 0)
    def _():
        fh[0:2] = jnp.zeros((2, 4, W, L), BF16)

    clear_rows(fh)
    pre[...] = gather_columns(spread(fh, w1n))
    for b in range(3):
        ft[b] = fh[:, b : b + R].reshape(6 * R * W, L).astype(F32).T[:C].astype(BF16)
    st[...] = shifted_transposes(silu(pre[...]).astype(BF16).astype(F32))
    for copy in ups:
        copy.wait_recv()
    clear_late(uh)
    clear_rows(uh)

    def cross_cores(g):
        return remote(
            mine.at[g, pl.ds((1 - core) * HALF, HALF)], rc.at[g], cs.at[g], cr.at[g], sibling
        )

    grad = jnp.dot(
        st[...], jnp.concatenate(taps_of(uh), axis=1), preferred_element_type=F32
    )
    for n in range(9):
        mine[0, n * BLOCK : (n + 1) * BLOCK] = pack(grad[:, n * L : n * L + L]).astype(BF16)
    across_two = cross_cores(0)

    d_second = gather_columns(spread(uh, w2t, True))
    d_pre = (d_second * silu_slope(pre[...])).astype(BF16)
    dh[0:T, 1:3] = d_pre.reshape(T, R, W, L)
    downs = halo(dh, (0, 1), dh, 0, 0, 4, -1, 10)

    d_pre = d_pre.astype(F32)
    column = lax.broadcasted_iota(jnp.int32, (CELLS, L), 0) % W
    after = jnp.where(column == W - 1, 0.0, pltpu.roll(d_pre, CELLS - 1, 0))
    before = jnp.where(column == 0, 0.0, pltpu.roll(d_pre, 1, 0))
    moved = jnp.concatenate([after, d_pre, before], axis=1).astype(BF16)
    field = jnp.concatenate(
        [ft[b, :, a * R * W : a * R * W + CELLS] for a in range(3) for b in range(3)], axis=0
    )
    grad = jnp.dot(field, moved, preferred_element_type=F32)
    for a in range(3):
        for e in range(3):
            n = a * 3 + e
            mine[1, n * BLOCK : (n + 1) * BLOCK] = pack(
                grad[a * 3 * C : (a + 1) * 3 * C, e * L : e * L + L]
            ).astype(BF16)
    across_one = cross_cores(1)

    def drain(ref, sem):
        pltpu.make_async_copy(ref, ref, sem).wait()

    def total_of(parts):
        total = parts[0].astype(F32)
        for part in parts[1:]:
            total = total + part.astype(F32)
        return total

    def rows_at(start, size):
        return pl.ds(pl.multiple_of(start, SHARE), size)

    def scatter(g, across):
        across.wait_recv()

        def add(spot):
            own = pl.ds(pl.multiple_of(core * HALF + spot.start, SHARE), spot.size)
            held[g, spot] = total_of([mine[g, own], rc[g, spot]]).astype(BF16)

        for k in (4, 3, 5, -2, -1, -3, 2, 6, 1, 7):
            if k > 0:
                spot = rows_at((p + k) % 8 * CHUNK, CHUNK)
                add(spot)
                remote(held.at[g, spot], a1.at[g, k - 1], s1.at[0, g], q1.at[0, g], first_ring(k))
            else:
                spot = rows_at(PART + (x - k) % XN * WIDE, WIDE)
                add(spot)
                remote(held.at[g, spot], b1.at[g, -k - 1], s1.at[1, g], q1.at[1, g], third_ring(-k))
        add(rows_at(p * CHUNK, CHUNK))
        add(rows_at(PART + x * WIDE, WIDE))

    def second_scatter_x(g):
        drain(b1.at[g], q1.at[1, g])
        own = held[g, rows_at(PART + x * WIDE, WIDE)]
        pb[g] = total_of([own] + [b1[g, k] for k in range(3)]).astype(BF16)
        for k in FAR_FIRST:
            spot = pb.at[g, rows_at((p + k) % 8 * SHARE, SHARE)]
            remote(spot, b2.at[g, k - 1], s2.at[1, g], q2.at[1, g], first_ring(k))

    def second_scatter(g):
        drain(a1.at[g], q1.at[0, g])
        own = held[g, rows_at(p * CHUNK, CHUNK)]
        pa[g] = total_of([own] + [a1[g, k] for k in range(7)]).astype(BF16)
        for k in (2, 1, 3):
            spot = pa.at[g, rows_at((x + k) % XN * SHARE, SHARE)]
            remote(spot, a2.at[g, k - 1], s2.at[0, g], q2.at[0, g], third_ring(k))

    def second_reduce(g):
        drain(b2.at[g], q2.at[1, g])
        drain(a2.at[g], q2.at[0, g])
        own = pa[g, rows_at(x * SHARE, SHARE)]
        c2[g, q, 0:SHARE] = total_of([own] + [a2[g, k] for k in range(3)]).astype(BF16)
        own = pb[g, rows_at(p * SHARE, SHARE)]
        c2[g, q, SHARE : 2 * SHARE] = total_of([own] + [b2[g, k] for k in range(7)]).astype(BF16)
        slot = c2.at[g, q]
        for k in FAR_FIRST:
            remote(slot, slot, s3.at[g], q3.at[g], second_ring(k))

    def third_gather(g):
        drain(c2.at[g, pl.ds(0, 7)], q3.at[g])
        total = total_of([c2[g, k] for k in range(8)]).astype(BF16)
        start = core * HALF
        spot = fin.at[g, rows_at(start + PART + x * WIDE + p * SHARE, SHARE)]
        spot[...] = total[SHARE:]
        for k in FAR_FIRST:
            remote(spot, spot, s4.at[1, g], q4.at[1, g], first_ring(k))
        spot = fin.at[g, rows_at(start + p * CHUNK + x * SHARE, SHARE)]
        spot[...] = total[:SHARE]
        for k in (2, 1, 3):
            remote(spot, spot, s4.at[0, g], q4.at[0, g], third_ring(k))

    def gather(g):
        drain(fin.at[g, pl.ds(0, 3 * SHARE)], q4.at[0, g])
        spot = fin.at[g, rows_at(core * HALF + p * CHUNK, CHUNK)]
        for k in FAR_FIRST:
            remote(spot, spot, s6.at[0, g], q6.at[0, g], first_ring(k))

    def gather_x(g):
        drain(fin.at[g, pl.ds(0, 7 * SHARE)], q4.at[1, g])
        spot = fin.at[g, rows_at(core * HALF + PART + x * WIDE, WIDE)]
        for k in (2, 1, 3):
            remote(spot, spot, s6.at[1, g], q6.at[1, g], third_ring(k))

    def half_of(g, c):
        return fin.at[g, pl.ds(pl.multiple_of(c * HALF, HALF), HALF)]

    def store(g, c, n):
        spot = packed.at[g, pl.ds(pl.multiple_of(c * HALF, HALF), HALF)]
        copy = pltpu.make_async_copy(half_of(g, c), spot, oc.at[2 * g + n])
        copy.start()
        return copy

    def cross_back(g):
        drain(fin.at[g, pl.ds(0, 7 * CHUNK)], q6.at[0, g])
        drain(fin.at[g, pl.ds(0, 3 * WIDE)], q6.at[1, g])
        remote(half_of(g, core), half_of(g, core), s5.at[g], q5.at[g], sibling)
        return store(g, core, 0)

    def complete(g):
        drain(half_of(g, 1 - core), q5.at[g])
        return store(g, 1 - core, 1)

    pl.semaphore_wait(waves[1], len(twos))
    scatter(0, across_two)
    scatter(1, across_one)
    place_taps(w1t, w1, True)
    second_scatter_x(0)
    second_scatter_x(1)
    second_scatter(0)
    second_scatter(1)
    second_reduce(0)
    second_reduce(1)
    for copy in downs:
        copy.wait_recv()
    clear_late(dh)
    clear_rows(dh)
    d_first = gather_columns(spread(dh, w1t, True)).reshape(T, R, W, L)
    for t in range(T):
        for r in range(R):
            out_lat[t, r] = (
                up[t, r + 1].astype(F32)
                + d_first[t, r][:, :C] * silu_slope(lat[t + 2, r + 1].astype(F32))
            ).astype(BF16)
    stores = [pltpu.make_async_copy(out_lat, lat_out, oc.at[4])]
    stores[0].start()
    third_gather(0)
    third_gather(1)
    gather(0)
    gather(1)
    gather_x(0)
    gather_x(1)
    stores.append(cross_back(0))
    stores.append(cross_back(1))
    stores.append(complete(0))
    stores.append(complete(1))

    for copy in firsts + ups + downs + [across_two, across_one]:
        copy.wait_send()
    for g in range(2):
        drain(a1.at[g], s1.at[0, g])
        drain(b1.at[g], s1.at[1, g])
        drain(a2.at[g], s2.at[0, g])
        drain(b2.at[g], s2.at[1, g])
        drain(c2.at[g, pl.ds(0, 7)], s3.at[g])
        drain(fin.at[g, pl.ds(0, 3 * SHARE)], s4.at[0, g])
        drain(fin.at[g, pl.ds(0, 7 * SHARE)], s4.at[1, g])
        drain(fin.at[g, pl.ds(0, 7 * CHUNK)], s6.at[0, g])
        drain(fin.at[g, pl.ds(0, 3 * WIDE)], s6.at[1, g])
        drain(half_of(g, core), s5.at[g])
    for copy in stores:
        copy.wait()


def finish(packed, lat, out_lat, out_one, out_two, held, full, carried, ins, outs):
    fetches = []
    for n in range(6):
        spot = pl.ds(n % 3 * 3 * BLOCK, 3 * BLOCK)
        fetches.append(
            pltpu.make_async_copy(packed.at[n // 3, spot], held.at[n // 3, spot], ins.at[n])
        )
        fetches[-1].start()
    fetches.append(pltpu.make_async_copy(lat, carried, ins.at[6]))
    fetches[-1].start()
    copies = []

    def widened(g, n):
        return unpack(held[g, n * BLOCK : n * BLOCK + 216].astype(F32) * (1.0 / 512.0))

    def write(src, dst):
        copies.append(pltpu.make_async_copy(src, dst, outs.at[len(copies)]))
        copies[-1].start()

    for a in range(3):
        fetches[a].wait()
        for b in range(3):
            grad = widened(0, a * 3 + b)
            for e in range(3):
                full[0, ((2 - a) * 3 + 2 - b) * 3 + 2 - e] = grad[e * C : e * C + C, :C]
        spot = pl.ds((2 - a) * 9, 9)
        write(full.at[0, spot], out_two.at[spot])
    for a in range(3):
        fetches[3 + a].wait()
        for e in range(3):
            grad = widened(1, a * 3 + e)
            for b in range(3):
                full[1, (a * 3 + b) * 3 + e] = grad[b * C : b * C + C, :C]
        spot = pl.ds(a * 9, 9)
        write(full.at[1, spot], out_one.at[spot])
    fetches[6].wait()
    write(carried, out_lat)
    for copy in copies:
        copy.wait()


def local(latents, upstream, conv_one, conv_two):
    hbm = pl.BlockSpec(memory_space=pltpu.HBM)
    dma = pltpu.SemaphoreType.DMA
    grad = jax.ShapeDtypeStruct((27, C, C), F32)
    field = pltpu.VMEM(latents.shape, BF16)
    raw = pltpu.VMEM((6, 4, W, C), BF16)
    taps = pltpu.VMEM((27, C, C), BF16)
    halo = pltpu.VMEM((6, 4, W, L), BF16)
    matrix = pltpu.VMEM((9 * L, 3 * L), BF16)
    turned = pltpu.VMEM((3 * L, 9 * L), BF16)
    params = functools.partial(pltpu.CompilerParams, vmem_limit_bytes=60 << 20)
    latent_grad, packed = pl.pallas_call(
        kernel,
        out_shape=(
            jax.ShapeDtypeStruct(latents.shape, BF16),
            jax.ShapeDtypeStruct((2, ROWS, L), BF16),
        ),
        in_specs=[hbm] * 4,
        out_specs=[hbm] * 2,
        scratch_shapes=[
            raw,
            raw,
            taps,
            taps,
            field,
            halo,
            halo,
            halo,
            pltpu.VMEM((3, C, 6 * R * W), BF16),
            pltpu.VMEM((3 * C, CELLS), BF16),
            matrix,
            turned,
            turned,
            pltpu.VMEM((CELLS, L), F32),
            pltpu.VMEM((2, ROWS, L), BF16),
            pltpu.VMEM((2, HALF, L), BF16),
            pltpu.VMEM((2, HALF, L), BF16),
            pltpu.VMEM((2, CHUNK, L), BF16),
            pltpu.VMEM((2, WIDE, L), BF16),
            pltpu.VMEM((2, 7, CHUNK, L), BF16),
            pltpu.VMEM((2, 3, WIDE, L), BF16),
            pltpu.VMEM((2, 3, SHARE, L), BF16),
            pltpu.VMEM((2, 7, SHARE, L), BF16),
            pltpu.VMEM((2, 8, 2 * SHARE, L), BF16),
            pltpu.VMEM((2, ROWS, L), BF16),
            dma((4,)),
            dma((5,)),
            dma((15,)),
            dma((15,)),
            *[dma((2,))] * 2,
            *[dma((2, 2))] * 8,
            *[dma((2,))] * 4,
            *[pltpu.SemaphoreType.REGULAR] * 2,
        ],
        compiler_params=params(collective_id=0, has_side_effects=True),
    )(latents, upstream, conv_one.reshape(27, C, C), conv_two.reshape(27, C, C))
    latent_grad, one, two = pl.pallas_call(
        finish,
        out_shape=(jax.ShapeDtypeStruct(latents.shape, BF16), grad, grad),
        in_specs=[hbm] * 2,
        out_specs=[hbm] * 3,
        scratch_shapes=[
            pltpu.VMEM((2, ROWS, L), BF16),
            pltpu.VMEM((2, 27, C, C), F32),
            field,
            dma((7,)),
            dma((7,)),
        ],
        compiler_params=params(),
    )(packed, latent_grad)
    shape = (3, 3, 3, C, C)
    return latent_grad, one.reshape(shape), two.reshape(shape)


def solution(mesh):
    return jax.shard_map(
        local,
        mesh=mesh,
        in_specs=(P("tm", "rows", None, None), P("tm", "rows", None, None), P(), P()),
        out_specs=(P("tm", "rows", None, None), P(), P()),
        check_vma=False,
    )
```

```python
import functools

import jax
import jax.numpy as jnp
from jax import lax
from jax.experimental import pallas as pl
from jax.experimental.pallas import tpu as pltpu
from jax.sharding import PartitionSpec as P

MESH = pl.DeviceIdType.MESH
F32, BF16 = jnp.float32, jnp.bfloat16
T, R, W, C, L = 4, 2, 64, 96, 128
CELLS = T * R * W
YN, ZN, XN = 8, 8, 4
ROWS = 2048
HALF = ROWS // 2
PART = HALF // 2
CHUNK = PART // 8
WIDE = PART // XN
SHARE = CHUNK // XN
BLOCK = 224
FAR_FIRST = (4, 3, 5, 2, 6, 1, 7)


def silu(v):
    return v / (1.0 + jnp.exp(-v))


def silu_slope(v):
    s = 1.0 / (1.0 + jnp.exp(-v))
    return s * (1.0 + v * (1.0 - s))


def widen(v):
    return jnp.concatenate([v, jnp.zeros((v.shape[0], L - C), v.dtype)], axis=1)


def taps_of(ref):
    return [ref[a : a + T, b : b + R].reshape(CELLS, L) for a in range(3) for b in range(3)]


def spread(ref, weights, turned=False):
    total = None
    for a in range(3):
        part = jnp.concatenate(
            [ref[a : a + T, b : b + R].reshape(CELLS, L) for b in range(3)], axis=1
        )
        if turned:
            matrix, depth = weights[:, a * 3 * L : (a + 1) * 3 * L], 1
        else:
            matrix, depth = weights[a * 3 * L : (a + 1) * 3 * L, :], 0
        term = lax.dot_general(
            part, matrix, (((1,), (depth,)), ((), ())), preferred_element_type=F32
        )
        total = term if total is None else total + term
    return total


def gather_columns(wide):
    column = lax.broadcasted_iota(jnp.int32, (CELLS, L), 0) % W
    low = jnp.where(column == 0, 0.0, pltpu.roll(wide[:, :L], 1, 0))
    high = jnp.where(column == W - 1, 0.0, pltpu.roll(wide[:, 2 * L :], CELLS - 1, 0))
    return low + wide[:, L : 2 * L] + high


def shifted_transposes(v):
    turned = v.T[:C]
    column = lax.broadcasted_iota(jnp.int32, (C, CELLS), 1) % W
    after = jnp.where(column == W - 1, 0.0, pltpu.roll(turned, CELLS - 1, 1))
    before = jnp.where(column == 0, 0.0, pltpu.roll(turned, 1, 1))
    return jnp.concatenate([after, turned, before], axis=0).astype(BF16)


def pack(grad):
    lane = lax.broadcasted_iota(jnp.int32, (72, L), 1)
    tail = grad[216:288]
    rows = []
    for k in range(3):
        moved = pltpu.roll(tail, (C - 32 * k) % L, 1)
        rows.append(jnp.where(lane < C, grad[72 * k : 72 * k + 72], moved))
    rows.append(jnp.zeros((BLOCK - 216, L), F32))
    return jnp.concatenate(rows, axis=0)


def unpack(held):
    lane = lax.broadcasted_iota(jnp.int32, (72, L), 1)
    parts = [
        pltpu.roll(held[72 * k : 72 * k + 72], (32 * k - C) % L, 1) for k in range(3)
    ]
    tail = jnp.where(lane < 32, parts[0], jnp.where(lane < 64, parts[1], parts[2]))
    return jnp.concatenate([held, tail], axis=0)


def kernel(
    lat_in, up_in, w1_in, w2_in, lat_out, packed,
    lat, up, w1, w2, out_lat,
    fh, uh, dh, ft, st, w1n, w1t, w2t, pre,
    mine, rc, held, pa, pb, a1, b1, a2, b2, c2, fin,
    lc, oc, hs, hr, cs, cr, s1, q1, s2, q2, s4, q4, s6, q6, s3, q3, s5, q5, *waves,
):
    tm, rw = lax.axis_index("tm"), lax.axis_index("rows")
    y, core, z, x = tm // 2, tm % 2, rw // XN, rw % XN

    def at(y2, c2, z2, x2):
        return ((y2 % YN) * 2 + c2, (z2 % ZN) * XN + x2 % XN)

    def near(dt, dr):
        return ((tm + dt) % 16, (rw + dr) % 32)

    def first_ring(k):
        return at(y + k * core, core, z + k * (1 - core), x)

    def second_ring(k):
        return at(y + k * (1 - core), core, z + k * core, x)

    def third_ring(k):
        return at(y, core, z, x + k)

    p = z + core * (y - z)
    q = y + core * (z - y)
    sibling = at(y, 1 - core, z, x)

    def greet(semaphore, partners):
        for who in partners:
            pl.semaphore_signal(semaphore, inc=1, device_id=who, device_id_type=MESH)

    barrier = pltpu.get_barrier_semaphore()
    around = [near(dt, dr) for dt, dr in ((-1, -1), (-1, 1), (1, -1), (1, 1), (0, -1), (0, 1), (-1, 0), (1, 0))]
    ones = [at(y - 1, core, z, x), at(y + 1, core, z, x), at(y, core, z - 1, x), at(y, core, z + 1, x)]
    ones += [at(y, core, z, x - 1), at(y, core, z, x + 1)]
    twos = [at(y - 2, core, z, x), at(y + 2, core, z, x), at(y, core, z - 2, x), at(y, core, z + 2, x)]
    fetches = [
        pltpu.make_async_copy(src, dst, lc.at[n])
        for n, (src, dst) in enumerate(
            (
                (lat_in, lat.at[pl.ds(2, T), pl.ds(1, R)]),
                (up_in, up.at[pl.ds(0, T), pl.ds(1, R)]),
                (w1_in, w1),
                (w2_in, w2),
            )
        )
    ]
    fetches[0].start()
    fetches[1].start()
    greet(barrier, around + ones)
    fetches[2].start()
    fetches[3].start()

    def remote(src, dst, send, recv, who):
        copy = pltpu.make_async_remote_copy(
            src_ref=src, dst_ref=dst, send_sem=send, recv_sem=recv,
            device_id=who, device_id_type=MESH,
        )
        copy.start()
        return copy

    def halo(src, corner, dst, own, lead, to, step, base):
        copies = []
        for n, (dt, dr) in enumerate(((step, -1), (step, 1), (0, -1), (0, 1), (step, 0))):
            fs = pl.ds(corner[0] + lead, 2) if dt else pl.ds(corner[0], T)
            fd = pl.ds(to, 2) if dt else pl.ds(own, T)
            rs = pl.ds(corner[1], 2) if dr == 0 else pl.ds(corner[1] + (dr > 0), 1)
            rd = pl.ds(1, 2) if dr == 0 else pl.ds(3 if dr < 0 else 0, 1)
            copies.append(
                remote(src.at[fs, rs], dst.at[fd, rd], hs.at[base + n], hr.at[base + n], near(dt, dr))
            )
        return copies

    def take_lat(f, r):
        fh[f, r] = widen(silu(lat[f, r].astype(F32))).astype(BF16)

    def take_up(f, r):
        uh[f, r] = widen(up[f, r])

    lines = [(f, r) for f in range(6) for r in range(4)]
    own_lat = [(f, r) for f, r in lines if f >= 2 and r in (1, 2)]
    own_up = [(f, r) for f, r in lines if f < T and r in (1, 2)]
    fetches[0].wait()
    for line in own_lat:
        take_lat(*line)
    pl.semaphore_wait(barrier, len(around) + len(ones))
    firsts = halo(fh, (2, 1), fh, 2, 2, 0, 1, 0)
    fetches[1].wait()
    for line in own_up:
        take_up(*line)
    ups = halo(uh, (0, 1), uh, 0, 0, 4, -1, 5)
    greet(waves[0], ones)

    def place_taps(matrix, source, turned):
        matrix[...] = jnp.zeros_like(matrix)
        for a in range(3):
            for b in range(3):
                for e in range(3):
                    row, lane = (a * 3 + b) * L, e * L
                    if turned:
                        row, lane = (2 - e) * L, ((2 - a) * 3 + 2 - b) * L
                    matrix[row : row + C, lane : lane + C] = source[(a * 3 + b) * 3 + e]

    fetches[2].wait()
    place_taps(w1n, w1, False)
    fetches[3].wait()
    place_taps(w2t, w2, True)
    mine[:, 9 * BLOCK :] = jnp.zeros((2, ROWS - 9 * BLOCK, L), BF16)
    pl.semaphore_wait(waves[0], len(ones))
    greet(waves[1], twos)

    def clear_rows(ref):
        @pl.when(rw == 0)
        def _():
            ref[:, 0] = jnp.zeros((6, W, L), BF16)

        @pl.when(rw == 31)
        def _():
            ref[:, 3] = jnp.zeros((6, W, L), BF16)

    def clear_late(ref):
        @pl.when(tm == 15)
        def _():
            ref[4:6] = jnp.zeros((2, 4, W, L), BF16)

    for copy in firsts:
        copy.wait_recv()

    @pl.when(tm == 0)
    def _():
        fh[0:2] = jnp.zeros((2, 4, W, L), BF16)

    clear_rows(fh)
    pre[...] = gather_columns(spread(fh, w1n))
    for b in range(3):
        ft[b] = fh[:, b : b + R].reshape(6 * R * W, L).astype(F32).T[:C].astype(BF16)
    st[...] = shifted_transposes(silu(pre[...]).astype(BF16).astype(F32))
    for copy in ups:
        copy.wait_recv()
    clear_late(uh)
    clear_rows(uh)

    def cross_cores(g):
        return remote(
            mine.at[g, pl.ds((1 - core) * HALF, HALF)], rc.at[g], cs.at[g], cr.at[g], sibling
        )

    grad = jnp.dot(
        st[...], jnp.concatenate(taps_of(uh), axis=1), preferred_element_type=F32
    )
    for n in range(9):
        mine[0, n * BLOCK : (n + 1) * BLOCK] = pack(grad[:, n * L : n * L + L]).astype(BF16)
    across_two = cross_cores(0)

    d_second = gather_columns(spread(uh, w2t, True))
    d_pre = (d_second * silu_slope(pre[...])).astype(BF16)
    dh[0:T, 1:3] = d_pre.reshape(T, R, W, L)
    downs = halo(dh, (0, 1), dh, 0, 0, 4, -1, 10)

    d_pre = d_pre.astype(F32)
    column = lax.broadcasted_iota(jnp.int32, (CELLS, L), 0) % W
    after = jnp.where(column == W - 1, 0.0, pltpu.roll(d_pre, CELLS - 1, 0))
    before = jnp.where(column == 0, 0.0, pltpu.roll(d_pre, 1, 0))
    moved = jnp.concatenate([after, d_pre, before], axis=1).astype(BF16)
    field = jnp.concatenate(
        [ft[b, :, a * R * W : a * R * W + CELLS] for a in range(3) for b in range(3)], axis=0
    )
    grad = jnp.dot(field, moved, preferred_element_type=F32)
    for a in range(3):
        for e in range(3):
            n = a * 3 + e
            mine[1, n * BLOCK : (n + 1) * BLOCK] = pack(
                grad[a * 3 * C : (a + 1) * 3 * C, e * L : e * L + L]
            ).astype(BF16)
    across_one = cross_cores(1)

    def drain(ref, sem):
        pltpu.make_async_copy(ref, ref, sem).wait()

    def total_of(parts):
        total = parts[0].astype(F32)
        for part in parts[1:]:
            total = total + part.astype(F32)
        return total

    def rows_at(start, size):
        return pl.ds(pl.multiple_of(start, SHARE), size)

    def scatter(g, across):
        across.wait_recv()

        def add(spot):
            own = pl.ds(pl.multiple_of(core * HALF + spot.start, SHARE), spot.size)
            held[g, spot] = total_of([mine[g, own], rc[g, spot]]).astype(BF16)

        for k in (4, 3, 5, -2, -1, -3, 2, 6, 1, 7):
            if k > 0:
                spot = rows_at((p + k) % 8 * CHUNK, CHUNK)
                add(spot)
                remote(held.at[g, spot], a1.at[g, k - 1], s1.at[0, g], q1.at[0, g], first_ring(k))
            else:
                spot = rows_at(PART + (x - k) % XN * WIDE, WIDE)
                add(spot)
                remote(held.at[g, spot], b1.at[g, -k - 1], s1.at[1, g], q1.at[1, g], third_ring(-k))
        add(rows_at(p * CHUNK, CHUNK))
        add(rows_at(PART + x * WIDE, WIDE))

    def second_scatter_x(g):
        drain(b1.at[g], q1.at[1, g])
        own = held[g, rows_at(PART + x * WIDE, WIDE)]
        pb[g] = total_of([own] + [b1[g, k] for k in range(3)]).astype(BF16)
        for k in FAR_FIRST:
            spot = pb.at[g, rows_at((p + k) % 8 * SHARE, SHARE)]
            remote(spot, b2.at[g, k - 1], s2.at[1, g], q2.at[1, g], first_ring(k))

    def second_scatter(g):
        drain(a1.at[g], q1.at[0, g])
        own = held[g, rows_at(p * CHUNK, CHUNK)]
        pa[g] = total_of([own] + [a1[g, k] for k in range(7)]).astype(BF16)
        for k in (2, 1, 3):
            spot = pa.at[g, rows_at((x + k) % XN * SHARE, SHARE)]
            remote(spot, a2.at[g, k - 1], s2.at[0, g], q2.at[0, g], third_ring(k))

    def second_reduce(g):
        drain(b2.at[g], q2.at[1, g])
        drain(a2.at[g], q2.at[0, g])
        own = pa[g, rows_at(x * SHARE, SHARE)]
        c2[g, q, 0:SHARE] = total_of([own] + [a2[g, k] for k in range(3)]).astype(BF16)
        own = pb[g, rows_at(p * SHARE, SHARE)]
        c2[g, q, SHARE : 2 * SHARE] = total_of([own] + [b2[g, k] for k in range(7)]).astype(BF16)
        slot = c2.at[g, q]
        for k in FAR_FIRST:
            remote(slot, slot, s3.at[g], q3.at[g], second_ring(k))

    def third_gather(g):
        drain(c2.at[g, pl.ds(0, 7)], q3.at[g])
        total = total_of([c2[g, k] for k in range(8)]).astype(BF16)
        start = core * HALF
        spot = fin.at[g, rows_at(start + PART + x * WIDE + p * SHARE, SHARE)]
        spot[...] = total[SHARE:]
        for k in FAR_FIRST:
            remote(spot, spot, s4.at[1, g], q4.at[1, g], first_ring(k))
        spot = fin.at[g, rows_at(start + p * CHUNK + x * SHARE, SHARE)]
        spot[...] = total[:SHARE]
        for k in (2, 1, 3):
            remote(spot, spot, s4.at[0, g], q4.at[0, g], third_ring(k))

    def gather(g):
        drain(fin.at[g, pl.ds(0, 3 * SHARE)], q4.at[0, g])
        spot = fin.at[g, rows_at(core * HALF + p * CHUNK, CHUNK)]
        for k in FAR_FIRST:
            remote(spot, spot, s6.at[0, g], q6.at[0, g], first_ring(k))

    def gather_x(g):
        drain(fin.at[g, pl.ds(0, 7 * SHARE)], q4.at[1, g])
        spot = fin.at[g, rows_at(core * HALF + PART + x * WIDE, WIDE)]
        for k in (2, 1, 3):
            remote(spot, spot, s6.at[1, g], q6.at[1, g], third_ring(k))

    def half_of(g, c):
        return fin.at[g, pl.ds(pl.multiple_of(c * HALF, HALF), HALF)]

    def store(g):
        spot = packed.at[g, rows_at(core * HALF, HALF)]
        copy = pltpu.make_async_copy(half_of(g, core), spot, oc.at[g])
        copy.start()
        return copy

    def cross_part(g, start, sem):
        spot = rows_at(core * HALF + start, PART)
        remote(fin.at[g, spot], packed.at[g, spot], s5.at[sem, g], q5.at[sem, g], sibling)

    def cross_back(g):
        drain(fin.at[g, pl.ds(0, 3 * WIDE)], q6.at[1, g])
        cross_part(g, PART, 1)
        drain(fin.at[g, pl.ds(0, 7 * CHUNK)], q6.at[0, g])
        cross_part(g, 0, 0)
        return store(g)

    def complete(g):
        for n in range(2):
            drain(packed.at[g, rows_at((1 - core) * HALF, PART)], q5.at[n, g])

    pl.semaphore_wait(waves[1], len(twos))
    scatter(0, across_two)
    scatter(1, across_one)
    place_taps(w1t, w1, True)
    second_scatter_x(0)
    second_scatter_x(1)
    second_scatter(0)
    second_scatter(1)
    second_reduce(0)
    second_reduce(1)
    for copy in downs:
        copy.wait_recv()
    clear_late(dh)
    clear_rows(dh)
    d_first = gather_columns(spread(dh, w1t, True)).reshape(T, R, W, L)
    for t in range(T):
        for r in range(R):
            out_lat[t, r] = (
                up[t, r + 1].astype(F32)
                + d_first[t, r][:, :C] * silu_slope(lat[t + 2, r + 1].astype(F32))
            ).astype(BF16)
    stores = [pltpu.make_async_copy(out_lat, lat_out, oc.at[2])]
    stores[0].start()
    third_gather(0)
    third_gather(1)
    gather(0)
    gather(1)
    gather_x(0)
    gather_x(1)
    stores.append(cross_back(0))
    stores.append(cross_back(1))
    complete(0)
    complete(1)

    for copy in firsts + ups + downs + [across_two, across_one]:
        copy.wait_send()
    for g in range(2):
        drain(a1.at[g], s1.at[0, g])
        drain(b1.at[g], s1.at[1, g])
        drain(a2.at[g], s2.at[0, g])
        drain(b2.at[g], s2.at[1, g])
        drain(c2.at[g, pl.ds(0, 7)], s3.at[g])
        drain(fin.at[g, pl.ds(0, 3 * SHARE)], s4.at[0, g])
        drain(fin.at[g, pl.ds(0, 7 * SHARE)], s4.at[1, g])
        drain(fin.at[g, pl.ds(0, 7 * CHUNK)], s6.at[0, g])
        drain(fin.at[g, pl.ds(0, 3 * WIDE)], s6.at[1, g])
        drain(fin.at[g, pl.ds(0, PART)], s5.at[0, g])
        drain(fin.at[g, pl.ds(0, PART)], s5.at[1, g])
    for copy in stores:
        copy.wait()


def finish(packed, lat, out_lat, out_one, out_two, held, full, carried, ins, outs):
    fetches = []
    for n in range(6):
        spot = pl.ds(n % 3 * 3 * BLOCK, 3 * BLOCK)
        fetches.append(
            pltpu.make_async_copy(packed.at[n // 3, spot], held.at[n // 3, spot], ins.at[n])
        )
        fetches[-1].start()
    fetches.append(pltpu.make_async_copy(lat, carried, ins.at[6]))
    fetches[-1].start()
    copies = []

    def widened(g, n):
        return unpack(held[g, n * BLOCK : n * BLOCK + 216].astype(F32) * (1.0 / 512.0))

    def write(src, dst):
        copies.append(pltpu.make_async_copy(src, dst, outs.at[len(copies)]))
        copies[-1].start()

    for a in range(3):
        fetches[a].wait()
        for b in range(3):
            grad = widened(0, a * 3 + b)
            for e in range(3):
                full[0, ((2 - a) * 3 + 2 - b) * 3 + 2 - e] = grad[e * C : e * C + C, :C]
        spot = pl.ds((2 - a) * 9, 9)
        write(full.at[0, spot], out_two.at[spot])
    for a in range(3):
        fetches[3 + a].wait()
        for e in range(3):
            grad = widened(1, a * 3 + e)
            for b in range(3):
                full[1, (a * 3 + b) * 3 + e] = grad[b * C : b * C + C, :C]
        spot = pl.ds(a * 9, 9)
        write(full.at[1, spot], out_one.at[spot])
    fetches[6].wait()
    write(carried, out_lat)
    for copy in copies:
        copy.wait()


def local(latents, upstream, conv_one, conv_two):
    hbm = pl.BlockSpec(memory_space=pltpu.HBM)
    dma = pltpu.SemaphoreType.DMA
    grad = jax.ShapeDtypeStruct((27, C, C), F32)
    field = pltpu.VMEM(latents.shape, BF16)
    raw = pltpu.VMEM((6, 4, W, C), BF16)
    taps = pltpu.VMEM((27, C, C), BF16)
    halo = pltpu.VMEM((6, 4, W, L), BF16)
    matrix = pltpu.VMEM((9 * L, 3 * L), BF16)
    turned = pltpu.VMEM((3 * L, 9 * L), BF16)
    params = functools.partial(pltpu.CompilerParams, vmem_limit_bytes=60 << 20)
    latent_grad, packed = pl.pallas_call(
        kernel,
        out_shape=(
            jax.ShapeDtypeStruct(latents.shape, BF16),
            jax.ShapeDtypeStruct((2, ROWS, L), BF16),
        ),
        in_specs=[hbm] * 4,
        out_specs=[hbm] * 2,
        scratch_shapes=[
            raw,
            raw,
            taps,
            taps,
            field,
            halo,
            halo,
            halo,
            pltpu.VMEM((3, C, 6 * R * W), BF16),
            pltpu.VMEM((3 * C, CELLS), BF16),
            matrix,
            turned,
            turned,
            pltpu.VMEM((CELLS, L), F32),
            pltpu.VMEM((2, ROWS, L), BF16),
            pltpu.VMEM((2, HALF, L), BF16),
            pltpu.VMEM((2, HALF, L), BF16),
            pltpu.VMEM((2, CHUNK, L), BF16),
            pltpu.VMEM((2, WIDE, L), BF16),
            pltpu.VMEM((2, 7, CHUNK, L), BF16),
            pltpu.VMEM((2, 3, WIDE, L), BF16),
            pltpu.VMEM((2, 3, SHARE, L), BF16),
            pltpu.VMEM((2, 7, SHARE, L), BF16),
            pltpu.VMEM((2, 8, 2 * SHARE, L), BF16),
            pltpu.VMEM((2, ROWS, L), BF16),
            dma((4,)),
            dma((3,)),
            dma((15,)),
            dma((15,)),
            *[dma((2,))] * 2,
            *[dma((2, 2))] * 8,
            *[dma((2,))] * 2,
            *[dma((2, 2))] * 2,
            *[pltpu.SemaphoreType.REGULAR] * 2,
        ],
        compiler_params=params(collective_id=0, has_side_effects=True),
    )(latents, upstream, conv_one.reshape(27, C, C), conv_two.reshape(27, C, C))
    latent_grad, one, two = pl.pallas_call(
        finish,
        out_shape=(jax.ShapeDtypeStruct(latents.shape, BF16), grad, grad),
        in_specs=[hbm] * 2,
        out_specs=[hbm] * 3,
        scratch_shapes=[
            pltpu.VMEM((2, ROWS, L), BF16),
            pltpu.VMEM((2, 27, C, C), F32),
            field,
            dma((7,)),
            dma((7,)),
        ],
        compiler_params=params(),
    )(packed, latent_grad)
    shape = (3, 3, 3, C, C)
    return latent_grad, one.reshape(shape), two.reshape(shape)


def solution(mesh):
    return jax.shard_map(
        local,
        mesh=mesh,
        in_specs=(P("tm", "rows", None, None), P("tm", "rows", None, None), P(), P()),
        out_specs=(P("tm", "rows", None, None), P(), P()),
        check_vma=False,
    )
```

```python
import functools

import jax
import jax.numpy as jnp
from jax import lax
from jax.experimental import pallas as pl
from jax.experimental.pallas import tpu as pltpu
from jax.sharding import PartitionSpec as P

MESH = pl.DeviceIdType.MESH
F32, BF16 = jnp.float32, jnp.bfloat16
T, R, W, C, L = 4, 2, 64, 96, 128
CELLS = T * R * W
YN, ZN, XN = 8, 8, 4
ROWS = 2048
HALF = ROWS // 2
PART = HALF // 2
CHUNK = PART // 8
WIDE = PART // XN
SHARE = CHUNK // XN
BLOCK = 224
FAR_FIRST = (4, 3, 5, 2, 6, 1, 7)


def silu(v):
    return v / (1.0 + jnp.exp(-v))


def silu_slope(v):
    s = 1.0 / (1.0 + jnp.exp(-v))
    return s * (1.0 + v * (1.0 - s))


def widen(v):
    return jnp.concatenate([v, jnp.zeros((v.shape[0], L - C), v.dtype)], axis=1)


def taps_of(ref):
    return [ref[a : a + T, b : b + R].reshape(CELLS, L) for a in range(3) for b in range(3)]


def spread(ref, weights, turned=False):
    total = None
    for a in range(3):
        part = jnp.concatenate(
            [ref[a : a + T, b : b + R].reshape(CELLS, L) for b in range(3)], axis=1
        )
        if turned:
            matrix, depth = weights[:, a * 3 * L : (a + 1) * 3 * L], 1
        else:
            matrix, depth = weights[a * 3 * L : (a + 1) * 3 * L, :], 0
        term = lax.dot_general(
            part, matrix, (((1,), (depth,)), ((), ())), preferred_element_type=F32
        )
        total = term if total is None else total + term
    return total


def gather_columns(wide):
    column = lax.broadcasted_iota(jnp.int32, (CELLS, L), 0) % W
    low = jnp.where(column == 0, 0.0, pltpu.roll(wide[:, :L], 1, 0))
    high = jnp.where(column == W - 1, 0.0, pltpu.roll(wide[:, 2 * L :], CELLS - 1, 0))
    return low + wide[:, L : 2 * L] + high


def shifted_transposes(v):
    turned = v.T[:C]
    column = lax.broadcasted_iota(jnp.int32, (C, CELLS), 1) % W
    after = jnp.where(column == W - 1, 0.0, pltpu.roll(turned, CELLS - 1, 1))
    before = jnp.where(column == 0, 0.0, pltpu.roll(turned, 1, 1))
    return jnp.concatenate([after, turned, before], axis=0).astype(BF16)


def pack(grad):
    lane = lax.broadcasted_iota(jnp.int32, (72, L), 1)
    tail = grad[216:288]
    rows = []
    for k in range(3):
        moved = pltpu.roll(tail, (C - 32 * k) % L, 1)
        rows.append(jnp.where(lane < C, grad[72 * k : 72 * k + 72], moved))
    rows.append(jnp.zeros((BLOCK - 216, L), F32))
    return jnp.concatenate(rows, axis=0)


def unpack(held):
    lane = lax.broadcasted_iota(jnp.int32, (72, L), 1)
    parts = [
        pltpu.roll(held[72 * k : 72 * k + 72], (32 * k - C) % L, 1) for k in range(3)
    ]
    tail = jnp.where(lane < 32, parts[0], jnp.where(lane < 64, parts[1], parts[2]))
    return jnp.concatenate([held, tail], axis=0)


def kernel(
    lat_in, up_in, w1_in, w2_in, lat_out, packed,
    lat, up, w1, w2, out_lat,
    fh, uh, dh, ft, st, w1n, w1t, w2t, pre,
    mine, rc, held, pa, pb, a1, b1, a2, b2, c2, fin,
    lc, oc, hs, hr, cs, cr, s1, q1, s2, q2, s4, q4, s6, q6, s3, q3, s5, q5, *waves,
):
    tm, rw = lax.axis_index("tm"), lax.axis_index("rows")
    y, core, z, x = tm // 2, tm % 2, rw // XN, rw % XN

    def at(y2, c2, z2, x2):
        return ((y2 % YN) * 2 + c2, (z2 % ZN) * XN + x2 % XN)

    def near(dt, dr):
        return ((tm + dt) % 16, (rw + dr) % 32)

    def first_ring(k):
        return at(y + k * core, core, z + k * (1 - core), x)

    def second_ring(k):
        return at(y + k * (1 - core), core, z + k * core, x)

    def third_ring(k):
        return at(y, core, z, x + k)

    p = z + core * (y - z)
    q = y + core * (z - y)
    sibling = at(y, 1 - core, z, x)

    def greet(semaphore, partners):
        for who in partners:
            pl.semaphore_signal(semaphore, inc=1, device_id=who, device_id_type=MESH)

    barrier = pltpu.get_barrier_semaphore()
    around = [near(dt, dr) for dt, dr in ((-1, -1), (-1, 1), (1, -1), (1, 1), (0, -1), (0, 1), (-1, 0), (1, 0))]
    ones = [at(y - 1, core, z, x), at(y + 1, core, z, x), at(y, core, z - 1, x), at(y, core, z + 1, x)]
    ones += [at(y, core, z, x - 1), at(y, core, z, x + 1)]
    twos = [at(y - 2, core, z, x), at(y + 2, core, z, x), at(y, core, z - 2, x), at(y, core, z + 2, x)]
    fetches = [
        pltpu.make_async_copy(src, dst, lc.at[n])
        for n, (src, dst) in enumerate(
            (
                (lat_in, lat.at[pl.ds(2, T), pl.ds(1, R)]),
                (up_in, up.at[pl.ds(0, T), pl.ds(1, R)]),
                (w1_in, w1),
                (w2_in, w2),
            )
        )
    ]
    fetches[0].start()
    fetches[1].start()
    greet(barrier, around + ones)
    fetches[2].start()
    fetches[3].start()

    def remote(src, dst, send, recv, who):
        copy = pltpu.make_async_remote_copy(
            src_ref=src, dst_ref=dst, send_sem=send, recv_sem=recv,
            device_id=who, device_id_type=MESH,
        )
        copy.start()
        return copy

    def halo(src, corner, dst, own, lead, to, step, base):
        copies = []
        for n, (dt, dr) in enumerate(((step, -1), (step, 1), (0, -1), (0, 1), (step, 0))):
            fs = pl.ds(corner[0] + lead, 2) if dt else pl.ds(corner[0], T)
            fd = pl.ds(to, 2) if dt else pl.ds(own, T)
            rs = pl.ds(corner[1], 2) if dr == 0 else pl.ds(corner[1] + (dr > 0), 1)
            rd = pl.ds(1, 2) if dr == 0 else pl.ds(3 if dr < 0 else 0, 1)
            copies.append(
                remote(src.at[fs, rs], dst.at[fd, rd], hs.at[base + n], hr.at[base + n], near(dt, dr))
            )
        return copies

    def take_lat(f, r):
        fh[f, r] = widen(silu(lat[f, r].astype(F32))).astype(BF16)

    def take_up(f, r):
        uh[f, r] = widen(up[f, r])

    lines = [(f, r) for f in range(6) for r in range(4)]
    own_lat = [(f, r) for f, r in lines if f >= 2 and r in (1, 2)]
    own_up = [(f, r) for f, r in lines if f < T and r in (1, 2)]
    fetches[0].wait()
    for line in own_lat:
        take_lat(*line)
    pl.semaphore_wait(barrier, len(around) + len(ones))
    firsts = halo(fh, (2, 1), fh, 2, 2, 0, 1, 0)
    fetches[1].wait()
    for line in own_up:
        take_up(*line)
    ups = halo(uh, (0, 1), uh, 0, 0, 4, -1, 5)
    greet(waves[0], ones)

    def place_taps(matrix, source, turned):
        matrix[...] = jnp.zeros_like(matrix)
        for a in range(3):
            for b in range(3):
                for e in range(3):
                    row, lane = (a * 3 + b) * L, e * L
                    if turned:
                        row, lane = (2 - e) * L, ((2 - a) * 3 + 2 - b) * L
                    matrix[row : row + C, lane : lane + C] = source[(a * 3 + b) * 3 + e]

    fetches[2].wait()
    place_taps(w1n, w1, False)
    fetches[3].wait()
    place_taps(w2t, w2, True)
    mine[:, 9 * BLOCK :] = jnp.zeros((2, ROWS - 9 * BLOCK, L), BF16)
    pl.semaphore_wait(waves[0], len(ones))
    greet(waves[1], twos)

    def clear_rows(ref):
        @pl.when(rw == 0)
        def _():
            ref[:, 0] = jnp.zeros((6, W, L), BF16)

        @pl.when(rw == 31)
        def _():
            ref[:, 3] = jnp.zeros((6, W, L), BF16)

    def clear_late(ref):
        @pl.when(tm == 15)
        def _():
            ref[4:6] = jnp.zeros((2, 4, W, L), BF16)

    for copy in firsts:
        copy.wait_recv()

    @pl.when(tm == 0)
    def _():
        fh[0:2] = jnp.zeros((2, 4, W, L), BF16)

    clear_rows(fh)
    pre[...] = gather_columns(spread(fh, w1n))
    for b in range(3):
        ft[b] = fh[:, b : b + R].reshape(6 * R * W, L).astype(F32).T[:C].astype(BF16)
    st[...] = shifted_transposes(silu(pre[...]).astype(BF16).astype(F32))
    for copy in ups:
        copy.wait_recv()
    clear_late(uh)
    clear_rows(uh)

    def cross_cores(g):
        return remote(
            mine.at[g, pl.ds((1 - core) * HALF, HALF)], rc.at[g], cs.at[g], cr.at[g], sibling
        )

    grad = jnp.dot(
        st[...], jnp.concatenate(taps_of(uh), axis=1), preferred_element_type=F32
    )
    for n in range(9):
        mine[0, n * BLOCK : (n + 1) * BLOCK] = pack(grad[:, n * L : n * L + L]).astype(BF16)
    across_two = cross_cores(0)

    d_second = gather_columns(spread(uh, w2t, True))
    d_pre = (d_second * silu_slope(pre[...])).astype(BF16)
    dh[0:T, 1:3] = d_pre.reshape(T, R, W, L)
    downs = halo(dh, (0, 1), dh, 0, 0, 4, -1, 10)

    d_pre = d_pre.astype(F32)
    column = lax.broadcasted_iota(jnp.int32, (CELLS, L), 0) % W
    after = jnp.where(column == W - 1, 0.0, pltpu.roll(d_pre, CELLS - 1, 0))
    before = jnp.where(column == 0, 0.0, pltpu.roll(d_pre, 1, 0))
    moved = jnp.concatenate([after, d_pre, before], axis=1).astype(BF16)
    field = jnp.concatenate(
        [ft[b, :, a * R * W : a * R * W + CELLS] for a in range(3) for b in range(3)], axis=0
    )
    grad = jnp.dot(field, moved, preferred_element_type=F32)
    for a in range(3):
        for e in range(3):
            n = a * 3 + e
            mine[1, n * BLOCK : (n + 1) * BLOCK] = pack(
                grad[a * 3 * C : (a + 1) * 3 * C, e * L : e * L + L]
            ).astype(BF16)
    across_one = cross_cores(1)

    def drain(ref, sem):
        pltpu.make_async_copy(ref, ref, sem).wait()

    def total_of(parts):
        total = parts[0].astype(F32)
        for part in parts[1:]:
            total = total + part.astype(F32)
        return total

    def rows_at(start, size):
        return pl.ds(pl.multiple_of(start, SHARE), size)

    def scatter(g, across):
        across.wait_recv()

        def add(spot):
            own = pl.ds(pl.multiple_of(core * HALF + spot.start, SHARE), spot.size)
            held[g, spot] = total_of([mine[g, own], rc[g, spot]]).astype(BF16)

        for k in (4, 3, 5, -2, -1, -3, 2, 6, 1, 7):
            if k > 0:
                spot = rows_at((p + k) % 8 * CHUNK, CHUNK)
                add(spot)
                remote(held.at[g, spot], a1.at[g, k - 1], s1.at[0, g], q1.at[0, g], first_ring(k))
            else:
                spot = rows_at(PART + (x - k) % XN * WIDE, WIDE)
                add(spot)
                remote(held.at[g, spot], b1.at[g, -k - 1], s1.at[1, g], q1.at[1, g], third_ring(-k))
        add(rows_at(p * CHUNK, CHUNK))
        add(rows_at(PART + x * WIDE, WIDE))

    def second_scatter_x(g):
        drain(b1.at[g], q1.at[1, g])
        own = held[g, rows_at(PART + x * WIDE, WIDE)]
        pb[g] = total_of([own] + [b1[g, k] for k in range(3)]).astype(BF16)
        for k in FAR_FIRST:
            spot = pb.at[g, rows_at((p + k) % 8 * SHARE, SHARE)]
            remote(spot, b2.at[g, k - 1], s2.at[1, g], q2.at[1, g], first_ring(k))

    def second_scatter(g):
        drain(a1.at[g], q1.at[0, g])
        own = held[g, rows_at(p * CHUNK, CHUNK)]
        pa[g] = total_of([own] + [a1[g, k] for k in range(7)]).astype(BF16)
        for k in (2, 1, 3):
            spot = pa.at[g, rows_at((x + k) % XN * SHARE, SHARE)]
            remote(spot, a2.at[g, k - 1], s2.at[0, g], q2.at[0, g], third_ring(k))

    def second_reduce(g):
        drain(b2.at[g], q2.at[1, g])
        drain(a2.at[g], q2.at[0, g])
        own = pa[g, rows_at(x * SHARE, SHARE)]
        c2[g, q, 0:SHARE] = total_of([own] + [a2[g, k] for k in range(3)]).astype(BF16)
        own = pb[g, rows_at(p * SHARE, SHARE)]
        c2[g, q, SHARE : 2 * SHARE] = total_of([own] + [b2[g, k] for k in range(7)]).astype(BF16)
        slot = c2.at[g, q]
        for k in FAR_FIRST:
            remote(slot, slot, s3.at[g], q3.at[g], second_ring(k))

    def third_gather(g):
        drain(c2.at[g, pl.ds(0, 7)], q3.at[g])
        total = total_of([c2[g, k] for k in range(8)]).astype(BF16)
        start = core * HALF
        spot = fin.at[g, rows_at(start + p * CHUNK + x * SHARE, SHARE)]
        spot[...] = total[:SHARE]
        for k in (2, 1, 3):
            remote(spot, spot, s4.at[0, g], q4.at[0, g], third_ring(k))
        spot = fin.at[g, rows_at(start + PART + x * WIDE + p * SHARE, SHARE)]
        spot[...] = total[SHARE:]
        for k in FAR_FIRST:
            remote(spot, spot, s4.at[1, g], q4.at[1, g], first_ring(k))

    def gather(g):
        drain(fin.at[g, pl.ds(0, 3 * SHARE)], q4.at[0, g])
        spot = fin.at[g, rows_at(core * HALF + p * CHUNK, CHUNK)]
        for k in FAR_FIRST:
            remote(spot, spot, s6.at[0, g], q6.at[0, g], first_ring(k))

    def gather_x(g):
        drain(fin.at[g, pl.ds(0, 7 * SHARE)], q4.at[1, g])
        spot = fin.at[g, rows_at(core * HALF + PART + x * WIDE, WIDE)]
        for k in (2, 1, 3):
            remote(spot, spot, s6.at[1, g], q6.at[1, g], third_ring(k))

    def half_of(g, c):
        return fin.at[g, pl.ds(pl.multiple_of(c * HALF, HALF), HALF)]

    def store(g):
        spot = packed.at[g, rows_at(core * HALF, HALF)]
        copy = pltpu.make_async_copy(half_of(g, core), spot, oc.at[g])
        copy.start()
        return copy

    def cross_part(g, start, sem):
        spot = rows_at(core * HALF + start, PART)
        remote(fin.at[g, spot], packed.at[g, spot], s5.at[sem, g], q5.at[sem, g], sibling)

    def cross_back(g):
        drain(fin.at[g, pl.ds(0, 3 * WIDE)], q6.at[1, g])
        cross_part(g, PART, 1)
        drain(fin.at[g, pl.ds(0, 7 * CHUNK)], q6.at[0, g])
        cross_part(g, 0, 0)
        return store(g)

    def complete(g):
        for n in range(2):
            drain(packed.at[g, rows_at((1 - core) * HALF, PART)], q5.at[n, g])

    pl.semaphore_wait(waves[1], len(twos))
    scatter(0, across_two)
    scatter(1, across_one)
    place_taps(w1t, w1, True)
    second_scatter_x(0)
    second_scatter_x(1)
    second_scatter(0)
    second_scatter(1)
    second_reduce(0)
    second_reduce(1)
    for copy in downs:
        copy.wait_recv()
    clear_late(dh)
    clear_rows(dh)
    d_first = gather_columns(spread(dh, w1t, True)).reshape(T, R, W, L)
    for t in range(T):
        for r in range(R):
            out_lat[t, r] = (
                up[t, r + 1].astype(F32)
                + d_first[t, r][:, :C] * silu_slope(lat[t + 2, r + 1].astype(F32))
            ).astype(BF16)
    stores = [pltpu.make_async_copy(out_lat, lat_out, oc.at[2])]
    stores[0].start()
    third_gather(0)
    third_gather(1)
    gather(0)
    gather(1)
    gather_x(0)
    gather_x(1)
    stores.append(cross_back(0))
    stores.append(cross_back(1))
    complete(0)
    complete(1)

    for copy in firsts + ups + downs + [across_two, across_one]:
        copy.wait_send()
    for g in range(2):
        drain(a1.at[g], s1.at[0, g])
        drain(b1.at[g], s1.at[1, g])
        drain(a2.at[g], s2.at[0, g])
        drain(b2.at[g], s2.at[1, g])
        drain(c2.at[g, pl.ds(0, 7)], s3.at[g])
        drain(fin.at[g, pl.ds(0, 3 * SHARE)], s4.at[0, g])
        drain(fin.at[g, pl.ds(0, 7 * SHARE)], s4.at[1, g])
        drain(fin.at[g, pl.ds(0, 7 * CHUNK)], s6.at[0, g])
        drain(fin.at[g, pl.ds(0, 3 * WIDE)], s6.at[1, g])
        drain(fin.at[g, pl.ds(0, PART)], s5.at[0, g])
        drain(fin.at[g, pl.ds(0, PART)], s5.at[1, g])
    for copy in stores:
        copy.wait()


def finish(packed, lat, out_lat, out_one, out_two, held, full, carried, ins, outs):
    fetches = []
    for n in range(6):
        spot = pl.ds(n % 3 * 3 * BLOCK, 3 * BLOCK)
        fetches.append(
            pltpu.make_async_copy(packed.at[n // 3, spot], held.at[n // 3, spot], ins.at[n])
        )
        fetches[-1].start()
    fetches.append(pltpu.make_async_copy(lat, carried, ins.at[6]))
    fetches[-1].start()
    copies = []

    def widened(g, n):
        return unpack(held[g, n * BLOCK : n * BLOCK + 216].astype(F32) * (1.0 / 512.0))

    def write(src, dst):
        copies.append(pltpu.make_async_copy(src, dst, outs.at[len(copies)]))
        copies[-1].start()

    for a in range(3):
        fetches[a].wait()
        for b in range(3):
            grad = widened(0, a * 3 + b)
            for e in range(3):
                full[0, ((2 - a) * 3 + 2 - b) * 3 + 2 - e] = grad[e * C : e * C + C, :C]
        spot = pl.ds((2 - a) * 9, 9)
        write(full.at[0, spot], out_two.at[spot])
    for a in range(3):
        fetches[3 + a].wait()
        for e in range(3):
            grad = widened(1, a * 3 + e)
            for b in range(3):
                full[1, (a * 3 + b) * 3 + e] = grad[b * C : b * C + C, :C]
        spot = pl.ds(a * 9, 9)
        write(full.at[1, spot], out_one.at[spot])
    fetches[6].wait()
    write(carried, out_lat)
    for copy in copies:
        copy.wait()


def local(latents, upstream, conv_one, conv_two):
    hbm = pl.BlockSpec(memory_space=pltpu.HBM)
    dma = pltpu.SemaphoreType.DMA
    grad = jax.ShapeDtypeStruct((27, C, C), F32)
    field = pltpu.VMEM(latents.shape, BF16)
    raw = pltpu.VMEM((6, 4, W, C), BF16)
    taps = pltpu.VMEM((27, C, C), BF16)
    halo = pltpu.VMEM((6, 4, W, L), BF16)
    matrix = pltpu.VMEM((9 * L, 3 * L), BF16)
    turned = pltpu.VMEM((3 * L, 9 * L), BF16)
    params = functools.partial(pltpu.CompilerParams, vmem_limit_bytes=60 << 20)
    latent_grad, packed = pl.pallas_call(
        kernel,
        out_shape=(
            jax.ShapeDtypeStruct(latents.shape, BF16),
            jax.ShapeDtypeStruct((2, ROWS, L), BF16),
        ),
        in_specs=[hbm] * 4,
        out_specs=[hbm] * 2,
        scratch_shapes=[
            raw,
            raw,
            taps,
            taps,
            field,
            halo,
            halo,
            halo,
            pltpu.VMEM((3, C, 6 * R * W), BF16),
            pltpu.VMEM((3 * C, CELLS), BF16),
            matrix,
            turned,
            turned,
            pltpu.VMEM((CELLS, L), F32),
            pltpu.VMEM((2, ROWS, L), BF16),
            pltpu.VMEM((2, HALF, L), BF16),
            pltpu.VMEM((2, HALF, L), BF16),
            pltpu.VMEM((2, CHUNK, L), BF16),
            pltpu.VMEM((2, WIDE, L), BF16),
            pltpu.VMEM((2, 7, CHUNK, L), BF16),
            pltpu.VMEM((2, 3, WIDE, L), BF16),
            pltpu.VMEM((2, 3, SHARE, L), BF16),
            pltpu.VMEM((2, 7, SHARE, L), BF16),
            pltpu.VMEM((2, 8, 2 * SHARE, L), BF16),
            pltpu.VMEM((2, ROWS, L), BF16),
            dma((4,)),
            dma((3,)),
            dma((15,)),
            dma((15,)),
            *[dma((2,))] * 2,
            *[dma((2, 2))] * 8,
            *[dma((2,))] * 2,
            *[dma((2, 2))] * 2,
            *[pltpu.SemaphoreType.REGULAR] * 2,
        ],
        compiler_params=params(collective_id=0, has_side_effects=True),
    )(latents, upstream, conv_one.reshape(27, C, C), conv_two.reshape(27, C, C))
    latent_grad, one, two = pl.pallas_call(
        finish,
        out_shape=(jax.ShapeDtypeStruct(latents.shape, BF16), grad, grad),
        in_specs=[hbm] * 2,
        out_specs=[hbm] * 3,
        scratch_shapes=[
            pltpu.VMEM((2, ROWS, L), BF16),
            pltpu.VMEM((2, 27, C, C), F32),
            field,
            dma((7,)),
            dma((7,)),
        ],
        compiler_params=params(),
    )(packed, latent_grad)
    shape = (3, 3, 3, C, C)
    return latent_grad, one.reshape(shape), two.reshape(shape)


def solution(mesh):
    return jax.shard_map(
        local,
        mesh=mesh,
        in_specs=(P("tm", "rows", None, None), P("tm", "rows", None, None), P(), P()),
        out_specs=(P("tm", "rows", None, None), P(), P()),
        check_vma=False,
    )
```
